256 devices in a mesh: mem: 4 (over x_hi, core), pts: 64 (over z, y, x_lo).
Axes of the slice: x: 4 (x_hi: 2, x_lo: 2; x = x_hi * 2 + x_lo), y: 4, z: 8, core: 2. Of those that a mesh axis runs over, the one named last changes fastest.
Arguments:
- hidden: bfloat16 [8, 1024, 65536], P('mem', None, 'pts'), may hold values from -16 to 16
- w_first: bfloat16 [1024, 1024], replicated, may hold values from -0.1875 to 0.1875
- b_first: float32 [1024], replicated, may hold values from -3 to 3
- w_out: bfloat16 [100, 1024], replicated, may hold values from -0.1875 to 0.1875
- target: float32 [100, 65536], P(None, 'pts'), may hold values from -6 to 6
- area: float32 [65536], P('pts'), may hold values from 0.3 to 3
- var_weight: float32 [100], replicated, may hold values from 1 to 10
Outputs:
- grad_hidden: bfloat16 [8, 1024, 65536], P('mem', None, 'pts')
- grad_w_first: float32 [1024, 1024], replicated
- grad_w_out: float32 [100, 1024], replicated
- grad_b_first: float32 [1024], replicated
The draws below stay inside these ranges and needn't reach their ends.
All inputs are finite; a program needn't handle non-finite values.
Results may differ from the reference program's by a relative error of at most 0.0084.
The reference program's roundings to bfloat16 on the way (of `act`, `grad_pred` and `grad_pre`) count: a program that leaves them out, or rounds other values in their place, can miss the bound.
Values sent between devices are 32-bit elements; how exact they have to be, the bound alone decides.
A program may use at most 128 MiB of HBM per device.

```python
import math
import jax
import jax.numpy as jnp
from jax import lax

H = 1024
V = 100
MEMBERS = 8
NPTS = 65536


def raised(values, rng, source, target, blocks, factor):
    owner, partner = [(jnp.arange(values.shape[dim]) // (values.shape[dim] // blocks)).reshape([-1 if axis == dim else 1 for axis in range(values.ndim)]) for dim in (source, target)]
    chosen = jax.random.permutation(rng, blocks)[partner]
    strong = (owner == chosen) | (owner == (partner + blocks // 2) % blocks)
    return jnp.where(strong, factor * values, values)


def levels(key, extent, pieces, smallest, high):
    loudness, own = 1.0, jax.random.fold_in(key, 6)
    for position, shards_of in pieces:
        draws = jnp.exp(jax.random.uniform(jax.random.fold_in(own, position), (shards_of,), jnp.float32, smallest / len(pieces), high / len(pieces)))
        loudness = loudness * jnp.repeat(draws, extent[position] // shards_of).reshape([-1 if axis == position else 1 for axis in range(len(extent))])
    return loudness


def gaussian(stream_key, shape, deviation, bound, cuts=(), kind=jnp.bfloat16):
    result = jax.random.normal(stream_key, shape, jnp.float32) * deviation
    if len(cuts) > 0:
        result = levels(stream_key, shape, cuts, -0.22, 0.18) * result
    return jnp.clip(result, min=-bound, max=bound).astype(kind)


def bell_draw_with(own_key, shape, width, bound, cuts, heavy, kind=jnp.bfloat16):
    array = width * jax.random.normal(own_key, shape, jnp.float32)
    if cuts:
        array = array * levels(own_key, shape, cuts, -0.22, 0.18)
    return jnp.clip(raised(array, jax.random.fold_in(own_key, 3), *heavy), -bound, bound).astype(kind)


def setup_inputs(seed: int = 0) -> dict:
    keys = jax.random.split(jax.random.key(seed), 8)
    return {
        "hidden": bell_draw_with(keys[0], (MEMBERS, H, NPTS), 1.0, 16.0, ((0, 4), (2, 64)), (2, 1, 64, 4.0)),
        "w_first": gaussian(keys[1], (H, H), H ** -0.5, 0.1875),
        "b_first": gaussian(keys[2], (H,), 0.5, 3.0, (), jnp.float32),
        "w_out": gaussian(keys[3], (V, H), H ** -0.5, 0.1875),
        "target": gaussian(keys[4], (V, NPTS), 1.0, 6.0, ((1, 64),), jnp.float32),
        "area": jnp.clip(jnp.exp(math.log(3.0) - 2.3025851 * jax.random.uniform(keys[5], (NPTS,), jnp.float32) ** levels(keys[5], (NPTS,), ((0, 64),), -0.2, 0.2)), 0.3, 3.0),
        "var_weight": jnp.clip(jnp.exp(jax.random.uniform(keys[6], (V,), jnp.float32, math.log(1.0), math.log(10.0))), 1.0, 10.0),
    }


curve = 0.044715
root_coef = 0.7978845608
delta_sq = 0.0025

def gelu_value(u):
    return 0.5 * u * (1.0 + jnp.tanh(root_coef * (u + curve * u * u * u)))

def gelu_slope(u):
    inner = jnp.tanh(root_coef * (u + curve * u * u * u))
    return 0.5 * (1.0 + inner) + 0.5 * u * (1.0 - inner * inner) * root_coef * (1.0 + 3.0 * curve * u * u)

def smooth_sign(d):
    return d / jnp.sqrt(d * d + delta_sq)

def reference(hidden, w_first, b_first, w_out, target, area, var_weight):
    scale = 1.0 / math.sqrt(MEMBERS * NPTS)
    eps_fair = 0.05 / MEMBERS
    pair_coef = (1.0 - eps_fair) / (MEMBERS * (MEMBERS - 1))

    def forward(member):
        pre = jnp.dot(w_first, member, preferred_element_type=jnp.float32) + b_first[:, None]
        act = gelu_value(pre).astype(jnp.bfloat16)
        return jnp.dot(w_out, act, preferred_element_type=jnp.float32)
    pred = lax.map(forward, hidden)
    pairs = jnp.zeros(pred.shape, jnp.float32)
    for other in range(MEMBERS):
        pairs = pairs + smooth_sign(pred - pred[other][None])
    weights = area[None, None, :] * var_weight[None, :, None]
    grad_pred = (weights * (smooth_sign(pred - target[None]) / MEMBERS - pair_coef * pairs)).astype(jnp.bfloat16)

    def backward(carry, items):
        member, grad_member = items
        pre = jnp.dot(w_first, member, preferred_element_type=jnp.float32) + b_first[:, None]
        act = gelu_value(pre).astype(jnp.bfloat16)
        grad_act = jnp.dot(w_out.T, grad_member, preferred_element_type=jnp.float32)
        grad_pre = (grad_act * gelu_slope(pre)).astype(jnp.bfloat16)
        grad_in = jnp.dot(w_first.T, grad_pre, preferred_element_type=jnp.float32).astype(jnp.bfloat16)
        sum_first = carry[0] + jnp.dot(grad_pre, member.T, preferred_element_type=jnp.float32)
        sum_out = carry[1] + jnp.dot(grad_member, act.T, preferred_element_type=jnp.float32)
        sum_bias = carry[2] + lax.optimization_barrier(jnp.sum(grad_pre.astype(jnp.float32), axis=1))
        return ((sum_first, sum_out, sum_bias), grad_in)
    start = (jnp.zeros((H, H), jnp.float32), jnp.zeros((V, H), jnp.float32), jnp.zeros((H,), jnp.float32))
    totals, grad_hidden = lax.scan(backward, start, (hidden, grad_pred))
    return (grad_hidden, totals[0] * scale, totals[1] * scale, totals[2] * scale)
```

```python
import math

import jax
import jax.numpy as jnp
from jax import lax
from jax.experimental import pallas as pl
from jax.experimental.pallas import tpu as pltpu
from jax.sharding import PartitionSpec as P

MESH = pl.DeviceIdType.MESH
f32 = jnp.float32
curve = 0.044715
root_coef = 0.7978845608
delta_sq = 0.0025


def gelu_value(u):
    return 0.5 * u * (1.0 + jnp.tanh(root_coef * (u + curve * u * u * u)))


def gelu_slope(u):
    inner = jnp.tanh(root_coef * (u + curve * u * u * u))
    return 0.5 * (1.0 + inner) + 0.5 * u * (1.0 - inner * inner) * root_coef * (
        1.0 + 3.0 * curve * u * u
    )


def smooth_sign(d):
    return d / jnp.sqrt(d * d + delta_sq)


def pair_terms(own, others):
    return jnp.sum(smooth_sign(own[:, None] - others[None]), axis=1)


def make_ar(NC, scale):
    pr = 32 // NC
    half = 16 * pr
    n = NC + 1

    def kern(gw, gs, ow, os, rcw, rcs, aw, as_, r1w, r1s, b1w, b1s, r2w, r2s, zw, zs, rzw, rzs,
             s_c, q_c, s_1, q_1, s_2, q_2, s_z, q_z, s_az, q_az, s_a2, q_a2, s_a1, q_a1, s_ac, q_ac):
        m = lax.axis_index("mem"); p = lax.axis_index("pts")
        c = m % 2
        x = (m // 2) * 2 + p % 2
        y = (p // 2) % 4
        z = p // 8
        def at(xx, yy, zz, cc):
            return ((xx // 2) * 2 + cc, (zz * 4 + yy) * 2 + xx % 2)
        def xo(d): return at((x + d) % 4, y, z, c)
        def yo(d): return at(x, (y + d) % 4, z, c)
        def zo(d): return at(x, y, (z + d) % 8, c)
        other = at(x, y, z, 1 - c)
        bar = pltpu.get_barrier_semaphore()
        peers = [other] + [xo(d) for d in (1, 2, 3)] + [yo(d) for d in (1, 2, 3)] + [zo(d) for d in range(1, 8)]
        for t in peers:
            pl.semaphore_signal(bar, inc=1, device_id=t, device_id_type=MESH)
        pl.semaphore_wait(bar, len(peers))
        sends = []
        def copy(src, dst, ss, rs, dev):
            cp = pltpu.make_async_remote_copy(src_ref=src, dst_ref=dst, send_sem=ss, recv_sem=rs, device_id=dev, device_id_type=MESH)
            cp.start(); sends.append(cp); return cp
        def mo(v, k): return pl.multiple_of(v, k)

        pend = {}
        def core_send(k):
            if k == 0:
                src, dst = gs.at[:, pl.ds(mo((1 - c) * 512, 512), 512)], rcs
            else:
                base = (k - 1) * 2 * half
                src, dst = gw.at[pl.ds(mo(base + (1 - c) * half, half), half)], rcw.at[k - 1]
            pend["c", k] = copy(src, dst, s_c.at[k], q_c.at[k], other)
        def st_core(k):
            pend["c", k].wait_recv()
            if k == 0:
                as_[...] = gs[:, pl.ds(mo(c * 512, 512), 512)] + rcs[...]
                a, r1, hw, q = as_, r1s, 256, 8
            else:
                base = (k - 1) * 2 * half
                aw[k - 1] = gw[pl.ds(mo(base + c * half, half), half)] + rcw[k - 1]
                a, r1, hw, q = aw.at[k - 1], r1w.at[k - 1], 512, pr
            for d in (2, 1, 3):
                xx = (x + d) % 4; yy = (y + d) % 4
                pend[1, k, 0, d] = copy(a.at[pl.ds(mo(xx * 4 * q, 4 * q), 4 * q), pl.ds(0, hw)], r1.at[0, d - 1], s_1.at[k, 0, d - 1], q_1.at[k, 0, d - 1], xo(d))
                pend[1, k, 1, d] = copy(a.at[pl.ds(mo(yy * 4 * q, 4 * q), 4 * q), pl.ds(hw, hw)], r1.at[1, d - 1], s_1.at[k, 1, d - 1], q_1.at[k, 1, d - 1], yo(d))
        def st_1(k):
            if k == 0:
                a, r1, b1, r2, hw, q = as_, r1s, b1s, r2s, 256, 8
            else:
                a, r1, b1, r2, hw, q = aw.at[k - 1], r1w.at[k - 1], b1w.at[k - 1], r2w.at[k - 1], 512, pr
            for h in (0, 1):
                me, nxt, dv = ((x, y, yo), (y, x, xo))[h]
                for d in (1, 2, 3):
                    pend[1, k, h, d].wait_recv()
                b1[h] = a[pl.ds(mo(me * 4 * q, 4 * q), 4 * q), pl.ds(h * hw, hw)] + r1[h, 0] + r1[h, 1] + r1[h, 2]
                for d in (2, 1, 3):
                    t = (nxt + d) % 4
                    pend[2, k, h, d] = copy(b1.at[h, pl.ds(mo(t * q, q), q)], r2.at[h, d - 1], s_2.at[k, h, d - 1], q_2.at[k, h, d - 1], dv(d))
        def st_2(k):
            if k == 0:
                b1, r2, zb, hw, q = b1s, r2s, zs, 256, 8
            else:
                b1, r2, zb, hw, q = b1w.at[k - 1], r2w.at[k - 1], zw.at[k - 1], 512, pr
            for h in (0, 1):
                nxt = (y, x)[h]
                for d in (1, 2, 3):
                    pend[2, k, h, d].wait_recv()
                zb[:, pl.ds(h * hw, hw)] = b1[h, pl.ds(mo(nxt * q, q), q)] + r2[h, 0] + r2[h, 1] + r2[h, 2]
            for d in (4, 3, 5, 2, 6, 1, 7):
                t = (z + d) % 8
                if k == 0:
                    src, dst = zs, rzs.at[d - 1]
                else:
                    src, dst = zw.at[k - 1, :, pl.ds(mo(t * 128, 128), 128)], rzw.at[k - 1, d - 1]
                pend["z", k, d] = copy(src, dst, s_z.at[k, d - 1], q_z.at[k, d - 1], zo(d))
        def piece_rows(k, h, q):
            j = (4 * x + y, 4 * y + x)[h]
            return j * q
        def st_z(k):
            for d in range(1, 8):
                pend["z", k, d].wait_recv()
            if k == 0:
                tot = zs[...]
                for d in range(7):
                    tot = tot + rzs[d]
                tot = tot * scale
                for h in (0, 1):
                    os[pl.ds(mo(piece_rows(k, h, 8), 8), 8), pl.ds(mo(c * 512 + h * 256, 256), 256)] = tot[:, h * 256:(h + 1) * 256]
                st_ag2(k)
            else:
                tot = zw[k - 1, :, pl.ds(mo(z * 128, 128), 128)]
                for d in range(7):
                    tot = tot + rzw[k - 1, d]
                hz = z // 4
                j = (1 - hz) * (4 * x + y) + hz * (4 * y + x)
                row = mo((k - 1) * 2 * half + c * half + j * pr, 8)
                dst = ow.at[pl.ds(row, pr), pl.ds(mo(z * 128, 128), 128)]
                dst[...] = tot * scale
                for d in (4, 3, 5, 2, 6, 1, 7):
                    pend["az", k, d] = copy(dst, dst, s_az.at[k, d - 1], q_az.at[k, d - 1], zo(d))
        def st_ag2(k):
            if k > 0:
                for d in range(1, 8):
                    pend["az", k, d].wait_recv()
            for h in (0, 1):
                dv = (yo, xo)[h]
                if k == 0:
                    blk = os.at[pl.ds(mo(piece_rows(k, h, 8), 8), 8), pl.ds(mo(c * 512 + h * 256, 256), 256)]
                else:
                    blk = ow.at[pl.ds(mo((k - 1) * 2 * half + c * half + piece_rows(k, h, pr), 8), pr), pl.ds(h * 512, 512)]
                for d in (2, 1, 3):
                    pend["a2", k, h, d] = copy(blk, blk, s_a2.at[k, h, d - 1], q_a2.at[k, h, d - 1], dv(d))
        def st_ag1(k):
            for h in (0, 1):
                for d in (1, 2, 3):
                    pend["a2", k, h, d].wait_recv()
                me, dv = ((x, xo), (y, yo))[h]
                if k == 0:
                    blk = os.at[pl.ds(mo(me * 32, 32), 32), pl.ds(mo(c * 512 + h * 256, 256), 256)]
                else:
                    blk = ow.at[pl.ds(mo((k - 1) * 2 * half + c * half + me * 4 * pr, 8), 4 * pr), pl.ds(h * 512, 512)]
                for d in (2, 1, 3):
                    pend["a1", k, h, d] = copy(blk, blk, s_a1.at[k, h, d - 1], q_a1.at[k, h, d - 1], dv(d))
        def st_agc(k):
            for h in (0, 1):
                for d in (1, 2, 3):
                    pend["a1", k, h, d].wait_recv()
            if k == 0:
                blk = os.at[:, pl.ds(mo(c * 512, 512), 512)]
            else:
                blk = ow.at[pl.ds(mo((k - 1) * 2 * half + c * half, half), half)]
            pend["ac", k] = copy(blk, blk, s_ac.at[k], q_ac.at[k], other)
        def nothing(k): pass
        def st_z_ag(k): pass
        for k in range(n):
            core_send(k)
        stages = [st_core, st_1, st_2, st_z, lambda k: st_ag2(k) if k else None, st_ag1, st_agc]
        for t in range(n + len(stages) - 1):
            for s in range(len(stages)):
                k = t - s
                if 0 <= k < n:
                    stages[s](k)
        for k in range(n):
            pend["ac", k].wait_recv()
        for cp in sends:
            cp.wait_send()

    V = pltpu.VMEM
    D = pltpu.SemaphoreType.DMA
    scratch = [V((NC, half, 1024), f32), V((128, 512), f32), V((NC, half, 1024), f32), V((128, 512), f32),
               V((NC, 2, 3, 4 * pr, 512), f32), V((2, 3, 32, 256), f32), V((NC, 2, 4 * pr, 512), f32), V((2, 32, 256), f32),
               V((NC, 2, 3, pr, 512), f32), V((2, 3, 8, 256), f32), V((NC, pr, 1024), f32), V((8, 512), f32),
               V((NC, 7, pr, 128), f32), V((7, 8, 512), f32)]
    for shp in ((n,), (n, 2, 3), (n, 2, 3), (n, 7), (n, 7), (n, 2, 3), (n, 2, 3), (n,)):
        scratch += [D(shp), D(shp)]
    return pl.pallas_call(kern, out_shape=(jax.ShapeDtypeStruct((1024, 1024), f32), jax.ShapeDtypeStruct((128, 1024), f32)),
        in_specs=[pl.BlockSpec(memory_space=pltpu.VMEM)] * 2, out_specs=[pl.BlockSpec(memory_space=pltpu.VMEM)] * 2,
        scratch_shapes=scratch, name=f"allreduce{NC}",
        compiler_params=pltpu.CompilerParams(collective_id=10 + NC, has_side_effects=True, vmem_limit_bytes=48 * 2**20))


def per_device(hidden, w_first, b_first, w_out, target, area, var_weight):
    mem_dev = hidden.shape[0]
    members = mem_dev * lax.axis_size("mem")
    total = members * hidden.shape[2] * lax.axis_size("pts")
    scale = 1.0 / math.sqrt(total)
    eps_fair = 0.05 / members
    pair_coef = (1.0 - eps_fair) / (members * (members - 1))
    pre = (
        jnp.einsum("oi,mip->mop", w_first, hidden, preferred_element_type=jnp.float32)
        + b_first[None, :, None]
    )
    act = gelu_value(pre).astype(jnp.bfloat16)
    pred = jnp.einsum("vh,mhp->mvp", w_out, act, preferred_element_type=jnp.float32)
    every = lax.all_gather(pred, "mem", axis=0, tiled=True)
    pairs = pair_terms(pred, every)
    weights = area[None, None, :] * var_weight[None, :, None]
    grad_pred = (weights * (smooth_sign(pred - target[None]) / members - pair_coef * pairs)).astype(
        jnp.bfloat16
    )
    grad_act = jnp.einsum("vh,mvp->mhp", w_out, grad_pred, preferred_element_type=jnp.float32)
    grad_pre = (grad_act * gelu_slope(pre)).astype(jnp.bfloat16)
    sum_first = jnp.einsum("mop,mip->oi", grad_pre, hidden, preferred_element_type=jnp.float32)
    sum_out = jnp.einsum("mvp,mhp->vh", grad_pred, act, preferred_element_type=jnp.float32)
    sum_bias = jnp.sum(grad_pre.astype(jnp.float32), axis=(0, 2))
    small = jnp.concatenate([sum_out, sum_bias[None], jnp.zeros((27, 1024), f32)], axis=0)
    sum_first, small = make_ar(4, scale)(sum_first, small)
    grad_hidden = jnp.einsum(
        "oi,mop->mip", w_first, grad_pre, preferred_element_type=jnp.float32
    ).astype(jnp.bfloat16)
    return (grad_hidden, sum_first, small[:100], small[100])


def solution(mesh):
    return jax.shard_map(
        per_device,
        mesh=mesh,
        in_specs=(P("mem", None, "pts"), P(), P(), P(), P(None, "pts"), P("pts"), P()),
        out_specs=(P("mem", None, "pts"), P(), P(), P()),
        check_vma=False,
    )
```

```python
import math

import jax
import jax.numpy as jnp
from jax import lax
from jax.experimental import pallas as pl
from jax.experimental.pallas import tpu as pltpu
from jax.sharding import PartitionSpec as P

MESH = pl.DeviceIdType.MESH
f32 = jnp.float32
bf16 = jnp.bfloat16
curve = 0.044715
root_coef = 0.7978845608
delta_sq = 0.0025
NQ = 4
CQ = 256
NC = 4
NT = (((1,), (1,)), ((), ()))


def smooth_sign(d):
    return d * lax.rsqrt(d * d + delta_sq)


def dot(a, b):
    return jnp.dot(a, b, preferred_element_type=f32)


def dot_nt(a, b):
    return lax.dot_general(a, b, NT, preferred_element_type=f32)


def make_kernel(members, pair_coef):
    pr = 32 // NC
    half = 16 * pr
    n = NC + 1

    def kern(hid_hbm, w, bcol, wo, tgt, area, vw, gh_hbm, ow_hbm, os_hbm,
             hid, wt, wot, act, slope, gpre, ghs, pred, pc, px, py, gpf, gp, bacc, gw, gs, ow, os,
             rcw, rcs, aw, as_, r1w, r1s, b1w, b1s, r2w, r2s, zw, zs, rzw, rzs,
             q_h, q_gh, q_ow, s_x, q_x, s_p, q_p, s_f, q_f,
             s_c, q_c, s_1, q_1, s_2, q_2, s_z, q_z, s_az, q_az, s_a2, q_a2, s_a1, q_a1, s_ac, q_ac):
        m = lax.axis_index("mem"); p = lax.axis_index("pts")
        c = m % 2
        x = (m // 2) * 2 + p % 2
        y = (p // 2) % 4
        z = p // 8
        def at(xx, yy, zz, cc):
            return ((xx // 2) * 2 + cc, (zz * 4 + yy) * 2 + xx % 2)
        def xo(d): return at((x + d) % 4, y, z, c)
        def yo(d): return at(x, (y + d) % 4, z, c)
        def zo(d): return at(x, y, (z + d) % 8, c)
        other = at(x, y, z, 1 - c)
        def mo(v, k): return pl.multiple_of(v, k)
        def cols(q): return pl.ds(mo(q * CQ, CQ), CQ)

        def load(q, i):
            return pltpu.make_async_copy(hid_hbm.at[i, :, cols(q)], hid.at[q, :, pl.ds(i * CQ, CQ)], q_h.at[q, i])
        def store(q, i):
            return pltpu.make_async_copy(ghs.at[q, :, pl.ds(i * CQ, CQ)], gh_hbm.at[i, :, cols(q)], q_gh.at[q, i])
        for q in range(NQ):
            for i in range(2):
                load(q, i).start()

        bar = pltpu.get_barrier_semaphore()
        peers = [other] + [xo(d) for d in (1, 2, 3)] + [yo(d) for d in (1, 2, 3)] + [zo(d) for d in range(1, 8)]
        for t in peers:
            pl.semaphore_signal(bar, inc=1, device_id=t, device_id_type=MESH)

        def remote(src, dst, ss, rs, dev):
            return pltpu.make_async_remote_copy(src_ref=src, dst_ref=dst, send_sem=ss, recv_sem=rs, device_id=dev, device_id_type=MESH)
        def cp_x(q): return remote(pred.at[q], px.at[q], s_x.at[q], q_x.at[q], xo(2))
        def cp_p(q): return remote(pred.at[q], pc.at[q], s_p.at[q], q_p.at[q], other)
        def cp_f(q): return remote(px.at[q], py.at[q], s_f.at[q], q_f.at[q], other)

        sends = []
        def copy(src, dst, ss, rs, dev):
            cp = remote(src, dst, ss, rs, dev)
            cp.start(); sends.append(cp); return cp
        pend = {}
        def core_send(k):
            if k == 0:
                src, dst = gs.at[:, pl.ds(mo((1 - c) * 512, 512), 512)], rcs
            else:
                base = (k - 1) * 2 * half
                src, dst = gw.at[pl.ds(mo(base + (1 - c) * half, half), half)], rcw.at[k - 1]
            pend["c", k] = copy(src, dst, s_c.at[k], q_c.at[k], other)
        def st_core(k):
            pend["c", k].wait_recv()
            if k == 0:
                as_[...] = gs[:, pl.ds(mo(c * 512, 512), 512)] + rcs[...]
                a, r1, hw, q = as_, r1s, 256, 8
            else:
                base = (k - 1) * 2 * half
                aw[k - 1] = gw[pl.ds(mo(base + c * half, half), half)] + rcw[k - 1]
                a, r1, hw, q = aw.at[k - 1], r1w.at[k - 1], 512, pr
            for d in (2, 1, 3):
                xx = (x + d) % 4; yy = (y + d) % 4
                pend[1, k, 0, d] = copy(a.at[pl.ds(mo(xx * 4 * q, 4 * q), 4 * q), pl.ds(0, hw)], r1.at[0, d - 1], s_1.at[k, 0, d - 1], q_1.at[k, 0, d - 1], xo(d))
                pend[1, k, 1, d] = copy(a.at[pl.ds(mo(yy * 4 * q, 4 * q), 4 * q), pl.ds(hw, hw)], r1.at[1, d - 1], s_1.at[k, 1, d - 1], q_1.at[k, 1, d - 1], yo(d))
        def st_1(k):
            if k == 0:
                a, r1, b1, r2, hw, q = as_, r1s, b1s, r2s, 256, 8
            else:
                a, r1, b1, r2, hw, q = aw.at[k - 1], r1w.at[k - 1], b1w.at[k - 1], r2w.at[k - 1], 512, pr
            for h in (0, 1):
                me, nxt, dv = ((x, y, yo), (y, x, xo))[h]
                for d in (1, 2, 3):
                    pend[1, k, h, d].wait_recv()
                b1[h] = a[pl.ds(mo(me * 4 * q, 4 * q), 4 * q), pl.ds(h * hw, hw)] + r1[h, 0] + r1[h, 1] + r1[h, 2]
                for d in (2, 1, 3):
                    t = (nxt + d) % 4
                    pend[2, k, h, d] = copy(b1.at[h, pl.ds(mo(t * q, q), q)], r2.at[h, d - 1], s_2.at[k, h, d - 1], q_2.at[k, h, d - 1], dv(d))
        def st_2(k):
            if k == 0:
                b1, r2, zb, hw, q = b1s, r2s, zs, 256, 8
            else:
                b1, r2, zb, hw, q = b1w.at[k - 1], r2w.at[k - 1], zw.at[k - 1], 512, pr
            for h in (0, 1):
                nxt = (y, x)[h]
                for d in (1, 2, 3):
                    pend[2, k, h, d].wait_recv()
                zb[:, pl.ds(h * hw, hw)] = b1[h, pl.ds(mo(nxt * q, q), q)] + r2[h, 0] + r2[h, 1] + r2[h, 2]
            for d in (4, 3, 5, 2, 6, 1, 7):
                t = (z + d) % 8
                if k == 0:
                    src, dst = zs, rzs.at[d - 1]
                else:
                    src, dst = zw.at[k - 1, :, pl.ds(mo(t * 128, 128), 128)], rzw.at[k - 1, d - 1]
                pend["z", k, d] = copy(src, dst, s_z.at[k, d - 1], q_z.at[k, d - 1], zo(d))
        def piece_rows(k, h, q):
            j = (4 * x + y, 4 * y + x)[h]
            return j * q
        def st_z(k):
            for d in range(1, 8):
                pend["z", k, d].wait_recv()
            if k == 0:
                tot = zs[...]
                for d in range(7):
                    tot = tot + rzs[d]
                tot = tot
                for h in (0, 1):
                    os[pl.ds(mo(piece_rows(k, h, 8), 8), 8), pl.ds(mo(c * 512 + h * 256, 256), 256)] = tot[:, h * 256:(h + 1) * 256]
                st_ag2(k)
            else:
                tot = zw[k - 1, :, pl.ds(mo(z * 128, 128), 128)]
                for d in range(7):
                    tot = tot + rzw[k - 1, d]
                hz = z // 4
                j = (1 - hz) * (4 * x + y) + hz * (4 * y + x)
                row = mo((k - 1) * 2 * half + c * half + j * pr, 8)
                dst = ow.at[pl.ds(row, pr), pl.ds(mo(z * 128, 128), 128)]
                dst[...] = tot
                for d in (4, 3, 5, 2, 6, 1, 7):
                    pend["az", k, d] = copy(dst, dst, s_az.at[k, d - 1], q_az.at[k, d - 1], zo(d))
        def st_ag2(k):
            if k > 0:
                for d in range(1, 8):
                    pend["az", k, d].wait_recv()
            for h in (0, 1):
                dv = (yo, xo)[h]
                if k == 0:
                    blk = os.at[pl.ds(mo(piece_rows(k, h, 8), 8), 8), pl.ds(mo(c * 512 + h * 256, 256), 256)]
                else:
                    blk = ow.at[pl.ds(mo((k - 1) * 2 * half + c * half + piece_rows(k, h, pr), 8), pr), pl.ds(h * 512, 512)]
                for d in (2, 1, 3):
                    pend["a2", k, h, d] = copy(blk, blk, s_a2.at[k, h, d - 1], q_a2.at[k, h, d - 1], dv(d))
        def st_ag1(k):
            for h in (0, 1):
                for d in (1, 2, 3):
                    pend["a2", k, h, d].wait_recv()
                me, dv = ((x, xo), (y, yo))[h]
                if k == 0:
                    blk = os.at[pl.ds(mo(me * 32, 32), 32), pl.ds(mo(c * 512 + h * 256, 256), 256)]
                else:
                    blk = ow.at[pl.ds(mo((k - 1) * 2 * half + c * half + me * 4 * pr, 8), 4 * pr), pl.ds(h * 512, 512)]
                for d in (2, 1, 3):
                    pend["a1", k, h, d] = copy(blk, blk, s_a1.at[k, h, d - 1], q_a1.at[k, h, d - 1], dv(d))
        def st_agc(k):
            for h in (0, 1):
                for d in (1, 2, 3):
                    pend["a1", k, h, d].wait_recv()
            if k == 0:
                blk = os.at[:, pl.ds(mo(c * 512, 512), 512)]
            else:
                blk = ow.at[pl.ds(mo((k - 1) * 2 * half + c * half, half), half)]
            pend["ac", k] = copy(blk, blk, s_ac.at[k], q_ac.at[k], other)
        def forward(q):
            for i in range(2):
                load(q, i).wait()
            for o in range(4):
                rows = pl.ds(o * 256, 256)
                u = dot(w[rows, :], hid[q]) + bcol[rows, :]
                u2 = u * u
                t = jnp.tanh(u * (root_coef + root_coef * curve * u2))
                h = 0.5 + 0.5 * t
                act[q, rows, :] = (u * h).astype(bf16)
                slope[q, rows, :] = h + (0.5 * root_coef) * u * (1.0 - t * t) * (1.0 + 3.0 * curve * u2)
            pred[q] = dot(wo[...], act[q])[:104]

        def grad_pred(q):
            def row(r, _):
                rr = pl.ds(mo(r * 8, 8), 8)
                a = pred[q, rr, :]
                s01 = smooth_sign(a[:, :CQ] - a[:, CQ:])
                pairs = jnp.concatenate([s01, -s01], axis=1)
                for ref in (pc, px, py):
                    v = ref[q, rr, :]
                    sw = jnp.concatenate([v[:, CQ:], v[:, :CQ]], axis=1)
                    pairs = pairs + (smooth_sign(a - v) + smooth_sign(a - sw))
                tg = tgt[rr, cols(q)]
                wt_ = vw[rr, :] * area[:, cols(q)]
                d = a - jnp.concatenate([tg, tg], axis=1)
                gpf[rr, :] = jnp.concatenate([wt_, wt_], axis=1) * (smooth_sign(d) * (1.0 / members) - pair_coef * pairs)
                return 0
            lax.fori_loop(0, 13, row, 0)
            gp[q] = gpf[...].astype(bf16)

        def back_pre(q):
            for o in range(4):
                rows = pl.ds(o * 256, 256)
                g = (dot(wot[rows, :], gp[q]) * slope[q, rows, :]).astype(bf16)
                gpre[q, rows, :] = g
                gf = g.astype(f32)
                bacc[rows, :] += (gf[:, :128] + gf[:, 128:256]) + (gf[:, 256:384] + gf[:, 384:])
            gs[:104, :] += dot_nt(gp[q], act[q])[:104]

        def back_w(q, o):
            rows = pl.ds(o * 256, 256)
            gw[rows, :] += dot_nt(gpre[q, rows, :], hid[q])

        def back_h(q):
            for o in range(4):
                rows = pl.ds(o * 256, 256)
                ghs[q, rows, :] = dot(wt[rows, :], gpre[q]).astype(bf16)
            for i in range(2):
                store(q, i).start()

        def fwd_step(q, _):
            forward(q)
            @pl.when(q == 0)
            def _():
                pl.semaphore_wait(bar, len(peers))
            cp_x(q).start()
            cp_p(q).start()
            return 0
        lax.fori_loop(0, NQ, fwd_step, 0)

        gw[...] = jnp.zeros((1024, 1024), f32)
        gs[...] = jnp.zeros((128, 1024), f32)
        bacc[...] = jnp.zeros((1024, 128), f32)
        gpf[...] = jnp.zeros((128, 2 * CQ), f32)
        for i in range(4):
            wt[pl.ds(i * 256, 256), :] = w[:, i * 256:(i + 1) * 256].T
        wot[...] = wo[...].T

        def arrive(q):
            cp_x(q).wait_recv()
            cp_f(q).start()
            cp_p(q).wait_recv()
            cp_f(q).wait_recv()
            grad_pred(q)
            back_pre(q)
        def bwd_step(q, _):
            arrive(q)
            for o in range(4):
                back_w(q, o)
            back_h(q)
            return 0
        lax.fori_loop(0, NQ - 1, bwd_step, 0)
        last = NQ - 1
        arrive(last)
        ones = jnp.ones((8, 128), f32)
        gs[104:112, :] = lax.dot_general(ones, bacc[...], NT, precision=lax.Precision.HIGHEST, preferred_element_type=f32)
        core_send(0)
        for k in range(1, n):
            back_w(last, k - 1)
            core_send(k)
        def st_out(k):
            pend["ac", k].wait_recv()
            if k == 0:
                cp = pltpu.make_async_copy(os, os_hbm, q_ow.at[0])
            else:
                rows = pl.ds((k - 1) * 2 * half, 2 * half)
                cp = pltpu.make_async_copy(ow.at[rows], ow_hbm.at[rows], q_ow.at[k])
            cp.start()
            pend["out", k] = cp
        stages = [st_core, st_1, st_2, st_z, lambda k: st_ag2(k) if k else None, st_ag1, st_agc, st_out]
        for t in range(n + len(stages) - 1):
            for s in range(len(stages)):
                k = t - s
                if 0 <= k < n:
                    stages[s](k)
            if t == 1:
                back_h(last)
        for k in range(n):
            pend["out", k].wait()
        for cp in sends:
            cp.wait_send()
        def finish(q, _):
            for i in range(2):
                store(q, i).wait()
            cp_x(q).wait_send()
            cp_p(q).wait_send()
            cp_f(q).wait_send()
            return 0
        lax.fori_loop(0, NQ, finish, 0)

    V = pltpu.VMEM
    D = pltpu.SemaphoreType.DMA
    W2 = 2 * CQ
    scratch = [V((NQ, 1024, W2), bf16), V((1024, 1024), bf16), V((1024, 128), bf16), V((NQ, 1024, W2), bf16), V((NQ, 1024, W2), f32),
               V((NQ, 1024, W2), bf16), V((NQ, 1024, W2), bf16),
               V((NQ, 104, W2), f32), V((NQ, 104, W2), f32), V((NQ, 104, W2), f32), V((NQ, 104, W2), f32),
               V((128, W2), f32), V((NQ, 128, W2), bf16), V((1024, 128), f32), V((1024, 1024), f32), V((128, 1024), f32),
               V((1024, 1024), f32), V((128, 1024), f32)]
    scratch += [V((NC, half, 1024), f32), V((128, 512), f32), V((NC, half, 1024), f32), V((128, 512), f32),
               V((NC, 2, 3, 4 * pr, 512), f32), V((2, 3, 32, 256), f32), V((NC, 2, 4 * pr, 512), f32), V((2, 32, 256), f32),
               V((NC, 2, 3, pr, 512), f32), V((2, 3, 8, 256), f32), V((NC, pr, 1024), f32), V((8, 512), f32),
               V((NC, 7, pr, 128), f32), V((7, 8, 512), f32)]
    scratch += [D((NQ, 2)), D((NQ, 2)), D((n,))] + [D((NQ,))] * 6
    for shp in ((n,), (n, 2, 3), (n, 2, 3), (n, 7), (n, 7), (n, 2, 3), (n, 2, 3), (n,)):
        scratch += [D(shp), D(shp)]
    vm = pl.BlockSpec(memory_space=pltpu.VMEM)
    hbm = pl.BlockSpec(memory_space=pl.ANY)
    return pl.pallas_call(kern,
        out_shape=(jax.ShapeDtypeStruct((2, 1024, 1024), bf16), jax.ShapeDtypeStruct((1024, 1024), f32), jax.ShapeDtypeStruct((128, 1024), f32)),
        in_specs=[hbm, vm, vm, vm, vm, vm, vm], out_specs=[hbm, hbm, hbm],
        scratch_shapes=scratch, name="fused",
        compiler_params=pltpu.CompilerParams(collective_id=3, has_side_effects=True, vmem_limit_bytes=60 * 2**20))


def per_device(hidden, w_first, b_first, w_out, target, area, var_weight):
    members = hidden.shape[0] * lax.axis_size("mem")
    total = members * hidden.shape[2] * lax.axis_size("pts")
    scale = 1.0 / math.sqrt(total)
    eps_fair = 0.05 / members
    pair_coef = (1.0 - eps_fair) / (members * (members - 1))
    wo = jnp.pad(w_out, ((0, 28), (0, 0)))
    tgt = jnp.pad(target, ((0, 4), (0, 0)))
    vw = jnp.pad(var_weight, (0, 4))[:, None]
    grad_hidden, ow, os = make_kernel(members, pair_coef)(hidden, w_first, b_first[:, None], wo, tgt, area[None], vw)
    return (grad_hidden, ow * scale, os[:100] * scale, os[104] * scale)


def solution(mesh):
    return jax.shard_map(
        per_device,
        mesh=mesh,
        in_specs=(P("mem", None, "pts"), P(), P(), P(), P(None, "pts"), P("pts"), P()),
        out_specs=(P("mem", None, "pts"), P(), P(), P()),
        check_vma=False,
    )
```

```python
import math

import jax
import jax.numpy as jnp
from jax import lax
from jax.experimental import pallas as pl
from jax.experimental.pallas import tpu as pltpu
from jax.sharding import PartitionSpec as P

MESH = pl.DeviceIdType.MESH
f32 = jnp.float32
bf16 = jnp.bfloat16
curve = 0.044715
root_coef = 0.7978845608
delta_sq = 0.0025
NQ = 4
CQ = 256
NC = 4
NT = (((1,), (1,)), ((), ()))
ORDER = (
    (0, 0), (0, 1), (1, 0), (9, 0), (9, 1), (9, 2), (9, 3), (0, 2), (1, 1), (2, 0), (9, 4), (9, 5), (9, 6), (9, 7),
    (0, 3), (1, 2), (2, 1), (3, 0), (9, 8), (9, 9), (9, 10), (9, 11), (0, 4), (1, 3), (2, 2), (3, 1), (4, 0),
    (9, 12), (9, 13), (9, 14), (9, 15), (1, 4), (2, 3), (3, 2), (4, 1), (5, 0), (9, 16), (9, 17), (9, 18), (9, 19),
    (2, 4), (3, 3), (4, 2), (5, 1), (6, 0), (3, 4), (4, 3), (5, 2), (6, 1), (7, 0), (4, 4), (5, 3), (6, 2), (7, 1),
    (5, 4), (6, 3), (7, 2), (6, 4), (7, 3), (7, 4),
)


def smooth_sign(d):
    return d * lax.rsqrt(d * d + delta_sq)


def dot(a, b):
    return jnp.dot(a, b, preferred_element_type=f32)


def dot_nt(a, b):
    return lax.dot_general(a, b, NT, preferred_element_type=f32)


def make_kernel(members, pair_coef, scale):
    pr = 32 // NC
    half = 16 * pr
    n = NC + 1

    def kern(hid_hbm, w, brow, wo_in, tgt_in, area, vwrow, ghs, ow, os,
             hid, wo, wot, bcol, vw, tgt, act, slope, pred, pc, px, py, gp, bacc, gw, gs,
             rcw, rcs, as_, r1w, r1s, b1w, b1s, r2w, r2s, zw, zs, rzw, rzs,
             q_h, s_x, q_x, s_p, q_p, s_f, q_f,
             s_c, q_c, s_1, q_1, s_2, q_2, s_z, q_z, s_az, q_az, s_a2, q_a2, s_a1, q_a1, s_ac, q_ac):
        m = lax.axis_index("mem"); p = lax.axis_index("pts")
        c = m % 2
        x = (m // 2) * 2 + p % 2
        y = (p // 2) % 4
        z = p // 8
        def at(xx, yy, zz, cc):
            return ((xx // 2) * 2 + cc, (zz * 4 + yy) * 2 + xx % 2)
        def xo(d): return at((x + d) % 4, y, z, c)
        def yo(d): return at(x, (y + d) % 4, z, c)
        def zo(d): return at(x, y, (z + d) % 8, c)
        other = at(x, y, z, 1 - c)
        def mo(v, k): return pl.multiple_of(v, k)
        def cols(q): return pl.ds(mo(q * CQ, CQ), CQ)

        def load(q, i):
            return pltpu.make_async_copy(hid_hbm.at[i, :, cols(q)], hid.at[q, :, pl.ds(i * CQ, CQ)], q_h.at[q, i])
        for q in range(NQ):
            for i in range(2):
                load(q, i).start()

        bar = pltpu.get_barrier_semaphore()
        peers = [other] + [xo(d) for d in (1, 2, 3)] + [yo(d) for d in (1, 2, 3)] + [zo(d) for d in range(1, 8)]
        for t in peers:
            pl.semaphore_signal(bar, inc=1, device_id=t, device_id_type=MESH)

        def remote(src, dst, ss, rs, dev):
            return pltpu.make_async_remote_copy(src_ref=src, dst_ref=dst, send_sem=ss, recv_sem=rs, device_id=dev, device_id_type=MESH)
        def cp_x(q): return remote(pred.at[q], px.at[q], s_x.at[q], q_x.at[q], xo(2))
        def cp_p(q): return remote(pred.at[q], pc.at[q], s_p.at[q], q_p.at[q], other)
        def cp_f(q): return remote(px.at[q], py.at[q], s_f.at[q], q_f.at[q], other)

        sends = []
        def copy(src, dst, ss, rs, dev):
            cp = remote(src, dst, ss, rs, dev)
            cp.start(); sends.append(cp); return cp
        pend = {}
        def core_send(k):
            if k == 0:
                src, dst = gs.at[:, pl.ds(mo((1 - c) * 512, 512), 512)], rcs
            else:
                base = (k - 1) * 2 * half
                src, dst = gw.at[pl.ds(mo(base + (1 - c) * half, half), half)], rcw.at[k - 1]
            pend["c", k] = copy(src, dst, s_c.at[k], q_c.at[k], other)
        def st_core(k):
            pend["c", k].wait_recv()
            if k == 0:
                as_[...] = gs[:, pl.ds(mo(c * 512, 512), 512)] + rcs[...]
                a, r1, hw, q = as_, r1s, 256, 8
            else:
                base = (k - 1) * 2 * half
                mine = gw.at[pl.ds(mo(base + c * half, half), half)]
                mine[...] += rcw[k - 1]
                a, r1, hw, q = mine, r1w.at[k - 1], 512, pr
            for d in (2, 1, 3):
                xx = (x + d) % 4; yy = (y + d) % 4
                pend[1, k, 0, d] = copy(a.at[pl.ds(mo(xx * 4 * q, 4 * q), 4 * q), pl.ds(0, hw)], r1.at[0, d - 1], s_1.at[k, 0, d - 1], q_1.at[k, 0, d - 1], xo(d))
                pend[1, k, 1, d] = copy(a.at[pl.ds(mo(yy * 4 * q, 4 * q), 4 * q), pl.ds(hw, hw)], r1.at[1, d - 1], s_1.at[k, 1, d - 1], q_1.at[k, 1, d - 1], yo(d))
        def st_1(k):
            if k == 0:
                a, r1, b1, r2, hw, q = as_, r1s, b1s, r2s, 256, 8
            else:
                base = (k - 1) * 2 * half
                a, r1, b1, r2, hw, q = gw.at[pl.ds(mo(base + c * half, half), half)], r1w.at[k - 1], b1w.at[k - 1], r2w.at[k - 1], 512, pr
            for h in (0, 1):
                me, nxt, dv = ((x, y, yo), (y, x, xo))[h]
                for d in (1, 2, 3):
                    pend[1, k, h, d].wait_recv()
                b1[h] = a[pl.ds(mo(me * 4 * q, 4 * q), 4 * q), pl.ds(h * hw, hw)] + r1[h, 0] + r1[h, 1] + r1[h, 2]
                for d in (2, 1, 3):
                    t = (nxt + d) % 4
                    pend[2, k, h, d] = copy(b1.at[h, pl.ds(mo(t * q, q), q)], r2.at[h, d - 1], s_2.at[k, h, d - 1], q_2.at[k, h, d - 1], dv(d))
        def st_2(k):
            if k == 0:
                b1, r2, zb, hw, q = b1s, r2s, zs, 256, 8
            else:
                b1, r2, zb, hw, q = b1w.at[k - 1], r2w.at[k - 1], zw.at[k - 1], 512, pr
            for h in (0, 1):
                nxt = (y, x)[h]
                for d in (1, 2, 3):
                    pend[2, k, h, d].wait_recv()
                zb[:, pl.ds(h * hw, hw)] = b1[h, pl.ds(mo(nxt * q, q), q)] + r2[h, 0] + r2[h, 1] + r2[h, 2]
            for d in (4, 3, 5, 2, 6, 1, 7):
                t = (z + d) % 8
                if k == 0:
                    src, dst = zs, rzs.at[d - 1]
                else:
                    src, dst = zw.at[k - 1, :, pl.ds(mo(t * 128, 128), 128)], rzw.at[k - 1, d - 1]
                pend["z", k, d] = copy(src, dst, s_z.at[k, d - 1], q_z.at[k, d - 1], zo(d))
        def piece_rows(k, h, q):
            j = (4 * x + y, 4 * y + x)[h]
            return j * q
        def st_z(k):
            for d in range(1, 8):
                pend["z", k, d].wait_recv()
            if k == 0:
                tot = zs[...]
                for d in range(7):
                    tot = tot + rzs[d]
                tot = tot * scale
                tot = tot
                for h in (0, 1):
                    os[pl.ds(mo(piece_rows(k, h, 8), 8), 8), pl.ds(mo(c * 512 + h * 256, 256), 256)] = tot[:, h * 256:(h + 1) * 256]
            else:
                tot = zw[k - 1, :, pl.ds(mo(z * 128, 128), 128)]
                for d in range(7):
                    tot = tot + rzw[k - 1, d]
                hz = z // 4
                j = (1 - hz) * (4 * x + y) + hz * (4 * y + x)
                row = mo((k - 1) * 2 * half + c * half + j * pr, 8)
                dst = ow.at[pl.ds(row, pr), pl.ds(mo(z * 128, 128), 128)]
                dst[...] = tot * scale
                for d in (4, 3, 5, 2, 6, 1, 7):
                    pend["az", k, d] = copy(dst, dst, s_az.at[k, d - 1], q_az.at[k, d - 1], zo(d))
        def st_ag2(k):
            if k > 0:
                for d in range(1, 8):
                    pend["az", k, d].wait_recv()
            for h in (0, 1):
                dv = (yo, xo)[h]
                if k == 0:
                    blk = os.at[pl.ds(mo(piece_rows(k, h, 8), 8), 8), pl.ds(mo(c * 512 + h * 256, 256), 256)]
                else:
                    blk = ow.at[pl.ds(mo((k - 1) * 2 * half + c * half + piece_rows(k, h, pr), 8), pr), pl.ds(h * 512, 512)]
                for d in (2, 1, 3):
                    pend["a2", k, h, d] = copy(blk, blk, s_a2.at[k, h, d - 1], q_a2.at[k, h, d - 1], dv(d))
        def st_ag1(k):
            for h in (0, 1):
                for d in (1, 2, 3):
                    pend["a2", k, h, d].wait_recv()
                me, dv = ((x, xo), (y, yo))[h]
                if k == 0:
                    blk = os.at[pl.ds(mo(me * 32, 32), 32), pl.ds(mo(c * 512 + h * 256, 256), 256)]
                else:
                    blk = ow.at[pl.ds(mo((k - 1) * 2 * half + c * half + me * 4 * pr, 8), 4 * pr), pl.ds(h * 512, 512)]
                for d in (2, 1, 3):
                    pend["a1", k, h, d] = copy(blk, blk, s_a1.at[k, h, d - 1], q_a1.at[k, h, d - 1], dv(d))
        def st_agc(k):
            for h in (0, 1):
                for d in (1, 2, 3):
                    pend["a1", k, h, d].wait_recv()
            if k == 0:
                blk = os.at[:, pl.ds(mo(c * 512, 512), 512)]
            else:
                blk = ow.at[pl.ds(mo((k - 1) * 2 * half + c * half, half), half)]
            pend["ac", k] = copy(blk, blk, s_ac.at[k], q_ac.at[k], other)
        def forward(q):
            for i in range(2):
                load(q, i).wait()
            for o in range(4):
                rows = pl.ds(o * 256, 256)
                bias = bcol[rows, :]
                u = dot(w[rows, :], hid[q]) + jnp.concatenate([bias] * 4, axis=1)
                u2 = u * u
                t = jnp.tanh(u * (root_coef + root_coef * curve * u2))
                h = 0.5 + 0.5 * t
                a = u * h
                act[q, rows, :] = a.astype(bf16)
                slope[q, rows, :] = h + (a - a * h) * (2.0 * root_coef + 6.0 * root_coef * curve * u2)
            pred[q] = dot(wo[...], act[q])[:104]

        def grad_pred(q):
            a = pred[q]
            s01 = smooth_sign(a[:, :CQ] - a[:, CQ:])
            pairs = jnp.concatenate([s01, -s01], axis=1)
            for ref in (pc, px, py):
                v = ref[q]
                sw = jnp.concatenate([v[:, CQ:], v[:, :CQ]], axis=1)
                pairs = pairs + (smooth_sign(a - v) + smooth_sign(a - sw))
            tg = tgt[:, cols(q)]
            va = vw[:104, :]
            ar = area[:, cols(q)]
            wts = jnp.concatenate([va] * 4, axis=1) * jnp.concatenate([ar, ar], axis=1)
            d = a - jnp.concatenate([tg, tg], axis=1)
            g = wts * (smooth_sign(d) * (1.0 / members) - pair_coef * pairs)
            gp[q] = jnp.concatenate([g, jnp.zeros((24, 2 * CQ), f32)], axis=0).astype(bf16)

        def back_pre(q):
            gs[:104, :] += dot_nt(gp[q], act[q])[:104]
            for o in range(4):
                rows = pl.ds(o * 256, 256)
                g = (dot(wot[rows, :], gp[q]) * slope[q, rows, :]).astype(bf16)
                act[q, rows, :] = g
                gf = g.astype(f32)
                bacc[rows, :] += (gf[:, :128] + gf[:, 128:256]) + (gf[:, 256:384] + gf[:, 384:])

        def back_w(q, o):
            rows = pl.ds(o * 256, 256)
            gw[rows, :] += dot_nt(act[q, rows, :], hid[q])

        def late(j):
            if j < 4:
                for i in range(2):
                    hid[i, pl.ds(j * 256, 256), :] = w[i * 512:(i + 1) * 512, j * 256:(j + 1) * 256].T
            else:
                q = (j - 4) // 4
                rows = pl.ds((j - 4) % 4 * 256, 256)
                ghs[q, rows, :] = (dot(hid[0, rows, :], act[q, :512, :]) + dot(hid[1, rows, :], act[q, 512:, :])).astype(bf16)

        bcol[...] = jnp.broadcast_to(brow[...], (128, 1024)).T
        vw[...] = jnp.zeros((128, 128), f32)
        vw[:, :100] = jnp.broadcast_to(vwrow[...], (128, 100))
        vw[...] = vw[...].T
        tgt[96:104, :] = jnp.zeros((8, 1024), f32)
        tgt[:100, :] = tgt_in[...]
        gs[...] = jnp.zeros((128, 1024), f32)
        gs[:100, :] = wo_in[...].astype(f32)
        wo[...] = gs[...].astype(bf16)
        wot[...] = gs[...].T.astype(bf16)
        gs[...] = jnp.zeros((128, 1024), f32)
        gw[...] = jnp.zeros((1024, 1024), f32)
        bacc[...] = jnp.zeros((1024, 128), f32)

        def fwd_step(q, _):
            forward(q)
            @pl.when(q == 0)
            def _():
                pl.semaphore_wait(bar, len(peers))
            cp_x(q).start()
            cp_p(q).start()
            return 0
        lax.fori_loop(0, NQ, fwd_step, 0)

        def arrive(q):
            cp_x(q).wait_recv()
            cp_f(q).start()
            cp_p(q).wait_recv()
            cp_f(q).wait_recv()
            grad_pred(q)
            back_pre(q)
        def bwd_step(q, _):
            arrive(q)
            for o in range(4):
                back_w(q, o)
            return 0
        lax.fori_loop(0, NQ - 1, bwd_step, 0)
        last = NQ - 1
        arrive(last)
        ones = jnp.ones((8, 128), f32)
        gs[104:112, :] = lax.dot_general(ones, bacc[...], NT, precision=lax.Precision.HIGHEST, preferred_element_type=f32)
        core_send(0)
        for k in range(1, n):
            back_w(last, k - 1)
            core_send(k)
        def st_out(k):
            pend["ac", k].wait_recv()
        steps = {0: st_core, 1: st_1, 2: st_2, 3: st_z, 4: st_ag2, 5: st_ag1, 6: st_agc, 7: st_out}
        for stage, k in ORDER:
            if stage == 9:
                late(k)
            else:
                steps[stage](k)
        for cp in sends:
            cp.wait_send()
        def finish(q, _):
            cp_x(q).wait_send()
            cp_p(q).wait_send()
            cp_f(q).wait_send()
            return 0
        lax.fori_loop(0, NQ, finish, 0)

    V = pltpu.VMEM
    D = pltpu.SemaphoreType.DMA
    W2 = 2 * CQ
    scratch = [V((NQ, 1024, W2), bf16), V((128, 1024), bf16), V((1024, 128), bf16),
               V((1024, 128), f32), V((128, 128), f32), V((104, 1024), f32),
               V((NQ, 1024, W2), bf16), V((NQ, 1024, W2), f32),
               V((NQ, 104, W2), f32), V((NQ, 104, W2), f32), V((NQ, 104, W2), f32), V((NQ, 104, W2), f32),
               V((NQ, 128, W2), bf16), V((1024, 128), f32), V((1024, 1024), f32), V((128, 1024), f32)]
    scratch += [V((NC, half, 1024), f32), V((128, 512), f32), V((128, 512), f32),
               V((NC, 2, 3, 4 * pr, 512), f32), V((2, 3, 32, 256), f32), V((NC, 2, 4 * pr, 512), f32), V((2, 32, 256), f32),
               V((NC, 2, 3, pr, 512), f32), V((2, 3, 8, 256), f32), V((NC, pr, 1024), f32), V((8, 512), f32),
               V((NC, 7, pr, 128), f32), V((7, 8, 512), f32)]
    scratch += [D((NQ, 2))] + [D((NQ,))] * 6
    for shp in ((n,), (n, 2, 3), (n, 2, 3), (n, 7), (n, 7), (n, 2, 3), (n, 2, 3), (n,)):
        scratch += [D(shp), D(shp)]
    vm = pl.BlockSpec(memory_space=pltpu.VMEM)
    hbm = pl.BlockSpec(memory_space=pl.ANY)
    return pl.pallas_call(kern,
        out_shape=(jax.ShapeDtypeStruct((NQ, 1024, W2), bf16), jax.ShapeDtypeStruct((1024, 1024), f32), jax.ShapeDtypeStruct((128, 1024), f32)),
        in_specs=[hbm, vm, vm, vm, vm, vm, vm], out_specs=[vm, vm, vm],
        scratch_shapes=scratch, name="fused",
        compiler_params=pltpu.CompilerParams(collective_id=3, has_side_effects=True, vmem_limit_bytes=41 * 2**20))


def place(ghs, ow, os):
    def kern(ghs, ow, os, gh, gw, go, gb, out, sem):
        out[...] = os[:100, :]
        cps = [pltpu.make_async_copy(ow, gw, sem.at[0]), pltpu.make_async_copy(out, go, sem.at[1])]
        for q in range(NQ):
            for i in range(2):
                cps.append(pltpu.make_async_copy(ghs.at[q, :, pl.ds(i * CQ, CQ)], gh.at[i, :, pl.ds(q * CQ, CQ)], sem.at[2 + 2 * q + i]))
        for cp in cps:
            cp.start()
        gb[...] = os[104:105, :]
        for cp in cps:
            cp.wait()
    vm = pl.BlockSpec(memory_space=pltpu.VMEM)
    hbm = pl.BlockSpec(memory_space=pl.ANY)
    return pl.pallas_call(kern, out_shape=(jax.ShapeDtypeStruct((2, 1024, 1024), bf16), jax.ShapeDtypeStruct((1024, 1024), f32),
                                           jax.ShapeDtypeStruct((100, 1024), f32), jax.ShapeDtypeStruct((1, 1024), f32)),
        in_specs=[vm, vm, vm], out_specs=[hbm, hbm, hbm, vm], scratch_shapes=[pltpu.VMEM((100, 1024), f32), pltpu.SemaphoreType.DMA((2 + 2 * NQ,))], name="place",
        compiler_params=pltpu.CompilerParams(has_side_effects=True, vmem_limit_bytes=2**20))(ghs, ow, os)


def per_device(hidden, w_first, b_first, w_out, target, area, var_weight):
    members = hidden.shape[0] * lax.axis_size("mem")
    total = members * hidden.shape[2] * lax.axis_size("pts")
    scale = 1.0 / math.sqrt(total)
    eps_fair = 0.05 / members
    pair_coef = (1.0 - eps_fair) / (members * (members - 1))
    ghs, ow, os = make_kernel(members, pair_coef, scale)(hidden, w_first, b_first[None], w_out, target, area[None], var_weight[None])
    grad_hidden, grad_first, grad_out, grad_bias = place(ghs, ow, os)
    return (grad_hidden, grad_first, grad_out, grad_bias[0])


def solution(mesh):
    return jax.shard_map(
        per_device,
        mesh=mesh,
        in_specs=(P("mem", None, "pts"), P(), P(), P(), P(None, "pts"), P("pts"), P()),
        out_specs=(P("mem", None, "pts"), P(), P(), P()),
        check_vma=False,
    )
```

```python
import math

import jax
import jax.numpy as jnp
from jax import lax
from jax.experimental import pallas as pl
from jax.experimental.pallas import tpu as pltpu
from jax.sharding import PartitionSpec as P

MESH = pl.DeviceIdType.MESH
f32 = jnp.float32
bf16 = jnp.bfloat16
curve = 0.044715
root_coef = 0.7978845608
delta_sq = 0.0025
NQ = 8
CQ = 128
NC = 4
NT = (((1,), (1,)), ((), ()))
ORDER = (
    (0, 0), (0, 1), (1, 0), (9, 0), (9, 1), (9, 2), (9, 3), (0, 2), (1, 1), (2, 0), (9, 4), (9, 5), (9, 6), (9, 7),
    (0, 3), (1, 2), (2, 1), (3, 0), (9, 8), (9, 9), (9, 10), (9, 11), (0, 4), (1, 3), (2, 2), (3, 1), (4, 0),
    (9, 12), (9, 13), (9, 14), (9, 15), (1, 4), (2, 3), (3, 2), (4, 1), (5, 0), (9, 16), (9, 17), (9, 18), (9, 19),
    (2, 4), (3, 3), (4, 2), (5, 1), (6, 0), (3, 4), (4, 3), (5, 2), (6, 1), (7, 0), (4, 4), (5, 3), (6, 2), (7, 1),
    (5, 4), (6, 3), (7, 2), (6, 4), (7, 3), (7, 4),
)


def smooth_sign(d):
    return d * lax.rsqrt(d * d + delta_sq)


def dot(a, b):
    return jnp.dot(a, b, preferred_element_type=f32)


def dot_nt(a, b):
    return lax.dot_general(a, b, NT, preferred_element_type=f32)


def make_kernel(members, pair_coef, scale):
    pr = 32 // NC
    half = 16 * pr
    n = NC + 1

    def kern(hid_hbm, w_hbm, b_hbm, wo_hbm, tgt_hbm, area_hbm, vw_hbm, ghs, ow, os,
             w, brow, wo_in, tgt_in, area, vwrow, hid, wo, wot, bcol, vw, tgt, act, slope, pred, pc, px, py, gp, bacc, gw, gs,
             rcw, rcs, as_, r1w, r1s, b1w, b1s, r2w, r2s, zw, zs, rzw, rzs,
             q_h, q_in, s_x, q_x, s_p, q_p, s_f, q_f,
             s_c, q_c, s_1, q_1, s_2, q_2, s_z, q_z, s_az, q_az, s_a2, q_a2, s_a1, q_a1, s_ac, q_ac):
        m = lax.axis_index("mem"); p = lax.axis_index("pts")
        c = m % 2
        x = (m // 2) * 2 + p % 2
        y = (p // 2) % 4
        z = p // 8
        def at(xx, yy, zz, cc):
            return ((xx // 2) * 2 + cc, (zz * 4 + yy) * 2 + xx % 2)
        def xo(d): return at((x + d) % 4, y, z, c)
        def yo(d): return at(x, (y + d) % 4, z, c)
        def zo(d): return at(x, y, (z + d) % 8, c)
        other = at(x, y, z, 1 - c)
        def mo(v, k): return pl.multiple_of(v, k)
        def cols(q): return pl.ds(mo(q * CQ, CQ), CQ)

        def load(q, i):
            return pltpu.make_async_copy(hid_hbm.at[i, :, cols(q)], hid.at[q, :, pl.ds(i * CQ, CQ)], q_h.at[q, i])
        small_in = [pltpu.make_async_copy(a, b, q_in.at[i]) for i, (a, b) in enumerate(
            ((b_hbm, brow), (vw_hbm, vwrow), (wo_hbm, wo_in), (tgt_hbm, tgt_in), (area_hbm, area), (w_hbm, w)))]
        for cp in small_in:
            cp.start()
        for q in range(NQ):
            for i in range(2):
                load(q, i).start()

        bar = pltpu.get_barrier_semaphore()
        peers = [other] + [xo(d) for d in (1, 2, 3)] + [yo(d) for d in (1, 2, 3)] + [zo(d) for d in range(1, 8)]
        for t in peers:
            pl.semaphore_signal(bar, inc=1, device_id=t, device_id_type=MESH)

        def remote(src, dst, ss, rs, dev):
            return pltpu.make_async_remote_copy(src_ref=src, dst_ref=dst, send_sem=ss, recv_sem=rs, device_id=dev, device_id_type=MESH)
        def cp_x(q): return remote(pred.at[q], px.at[q], s_x.at[q], q_x.at[q], xo(2))
        def cp_p(q): return remote(pred.at[q], pc.at[q], s_p.at[q], q_p.at[q], other)
        def cp_f(q): return remote(px.at[q], py.at[q], s_f.at[q], q_f.at[q], other)

        sends = []
        def copy(src, dst, ss, rs, dev):
            cp = remote(src, dst, ss, rs, dev)
            cp.start(); sends.append(cp); return cp
        pend = {}
        def core_send(k):
            if k == 0:
                src, dst = gs.at[:, pl.ds(mo((1 - c) * 512, 512), 512)], rcs
            else:
                base = (k - 1) * 2 * half
                src, dst = gw.at[pl.ds(mo(base + (1 - c) * half, half), half)], rcw.at[k - 1]
            pend["c", k] = copy(src, dst, s_c.at[k], q_c.at[k], other)
        def st_core(k):
            pend["c", k].wait_recv()
            if k == 0:
                as_[...] = gs[:, pl.ds(mo(c * 512, 512), 512)] + rcs[...]
                a, r1, hw, q = as_, r1s, 256, 8
            else:
                base = (k - 1) * 2 * half
                mine = gw.at[pl.ds(mo(base + c * half, half), half)]
                mine[...] += rcw[k - 1]
                a, r1, hw, q = mine, r1w.at[k - 1], 512, pr
            for d in (2, 1, 3):
                xx = (x + d) % 4; yy = (y + d) % 4
                pend[1, k, 0, d] = copy(a.at[pl.ds(mo(xx * 4 * q, 4 * q), 4 * q), pl.ds(0, hw)], r1.at[0, d - 1], s_1.at[k, 0, d - 1], q_1.at[k, 0, d - 1], xo(d))
                pend[1, k, 1, d] = copy(a.at[pl.ds(mo(yy * 4 * q, 4 * q), 4 * q), pl.ds(hw, hw)], r1.at[1, d - 1], s_1.at[k, 1, d - 1], q_1.at[k, 1, d - 1], yo(d))
        def st_1(k):
            if k == 0:
                a, r1, b1, r2, hw, q = as_, r1s, b1s, r2s, 256, 8
            else:
                base = (k - 1) * 2 * half
                a, r1, b1, r2, hw, q = gw.at[pl.ds(mo(base + c * half, half), half)], r1w.at[k - 1], b1w.at[k - 1], r2w.at[k - 1], 512, pr
            for h in (0, 1):
                me, nxt, dv = ((x, y, yo), (y, x, xo))[h]
                for d in (1, 2, 3):
                    pend[1, k, h, d].wait_recv()
                b1[h] = a[pl.ds(mo(me * 4 * q, 4 * q), 4 * q), pl.ds(h * hw, hw)] + r1[h, 0] + r1[h, 1] + r1[h, 2]
                for d in (2, 1, 3):
                    t = (nxt + d) % 4
                    pend[2, k, h, d] = copy(b1.at[h, pl.ds(mo(t * q, q), q)], r2.at[h, d - 1], s_2.at[k, h, d - 1], q_2.at[k, h, d - 1], dv(d))
        def st_2(k):
            if k == 0:
                b1, r2, zb, hw, q = b1s, r2s, zs, 256, 8
            else:
                b1, r2, zb, hw, q = b1w.at[k - 1], r2w.at[k - 1], zw.at[k - 1], 512, pr
            for h in (0, 1):
                nxt = (y, x)[h]
                for d in (1, 2, 3):
                    pend[2, k, h, d].wait_recv()
                zb[:, pl.ds(h * hw, hw)] = b1[h, pl.ds(mo(nxt * q, q), q)] + r2[h, 0] + r2[h, 1] + r2[h, 2]
            for d in (4, 3, 5, 2, 6, 1, 7):
                t = (z + d) % 8
                if k == 0:
                    src, dst = zs, rzs.at[d - 1]
                else:
                    src, dst = zw.at[k - 1, :, pl.ds(mo(t * 128, 128), 128)], rzw.at[k - 1, d - 1]
                pend["z", k, d] = copy(src, dst, s_z.at[k, d - 1], q_z.at[k, d - 1], zo(d))
        def piece_rows(k, h, q):
            j = (4 * x + y, 4 * y + x)[h]
            return j * q
        def st_z(k):
            for d in range(1, 8):
                pend["z", k, d].wait_recv()
            if k == 0:
                tot = zs[...]
                for d in range(7):
                    tot = tot + rzs[d]
                tot = tot * scale
                tot = tot
                for h in (0, 1):
                    os[pl.ds(mo(piece_rows(k, h, 8), 8), 8), pl.ds(mo(c * 512 + h * 256, 256), 256)] = tot[:, h * 256:(h + 1) * 256]
            else:
                tot = zw[k - 1, :, pl.ds(mo(z * 128, 128), 128)]
                for d in range(7):
                    tot = tot + rzw[k - 1, d]
                hz = z // 4
                j = (1 - hz) * (4 * x + y) + hz * (4 * y + x)
                row = mo((k - 1) * 2 * half + c * half + j * pr, 8)
                dst = ow.at[pl.ds(row, pr), pl.ds(mo(z * 128, 128), 128)]
                dst[...] = tot * scale
                for d in (4, 3, 5, 2, 6, 1, 7):
                    pend["az", k, d] = copy(dst, dst, s_az.at[k, d - 1], q_az.at[k, d - 1], zo(d))
        def st_ag2(k):
            if k > 0:
                for d in range(1, 8):
                    pend["az", k, d].wait_recv()
            for h in (0, 1):
                dv = (yo, xo)[h]
                if k == 0:
                    blk = os.at[pl.ds(mo(piece_rows(k, h, 8), 8), 8), pl.ds(mo(c * 512 + h * 256, 256), 256)]
                else:
                    blk = ow.at[pl.ds(mo((k - 1) * 2 * half + c * half + piece_rows(k, h, pr), 8), pr), pl.ds(h * 512, 512)]
                for d in (2, 1, 3):
                    pend["a2", k, h, d] = copy(blk, blk, s_a2.at[k, h, d - 1], q_a2.at[k, h, d - 1], dv(d))
        def st_ag1(k):
            for h in (0, 1):
                for d in (1, 2, 3):
                    pend["a2", k, h, d].wait_recv()
                me, dv = ((x, xo), (y, yo))[h]
                if k == 0:
                    blk = os.at[pl.ds(mo(me * 32, 32), 32), pl.ds(mo(c * 512 + h * 256, 256), 256)]
                else:
                    blk = ow.at[pl.ds(mo((k - 1) * 2 * half + c * half + me * 4 * pr, 8), 4 * pr), pl.ds(h * 512, 512)]
                for d in (2, 1, 3):
                    pend["a1", k, h, d] = copy(blk, blk, s_a1.at[k, h, d - 1], q_a1.at[k, h, d - 1], dv(d))
        def st_agc(k):
            for h in (0, 1):
                for d in (1, 2, 3):
                    pend["a1", k, h, d].wait_recv()
            if k == 0:
                blk = os.at[:, pl.ds(mo(c * 512, 512), 512)]
            else:
                blk = ow.at[pl.ds(mo((k - 1) * 2 * half + c * half, half), half)]
            pend["ac", k] = copy(blk, blk, s_ac.at[k], q_ac.at[k], other)
        def forward(q):
            for i in range(2):
                load(q, i).wait()
            for o in range(4):
                rows = pl.ds(o * 256, 256)
                bias = bcol[rows, :]
                u = dot(w[rows, :], hid[q]) + jnp.concatenate([bias, bias], axis=1)
                u2 = u * u
                t = jnp.tanh(u * (root_coef + root_coef * curve * u2))
                h = 0.5 + 0.5 * t
                a = u * h
                act[q, rows, :] = a.astype(bf16)
                slope[q, rows, :] = h + (a - a * h) * (2.0 * root_coef + 6.0 * root_coef * curve * u2)
            pred[q] = dot(wo[...], act[q])[:104]

        def grad_pred(q):
            a = pred[q]
            s01 = smooth_sign(a[:, :CQ] - a[:, CQ:])
            pairs = jnp.concatenate([s01, -s01], axis=1)
            for ref in (pc, px, py):
                v = ref[q]
                sw = jnp.concatenate([v[:, CQ:], v[:, :CQ]], axis=1)
                pairs = pairs + (smooth_sign(a - v) + smooth_sign(a - sw))
            tg = tgt[:, cols(q)]
            va = vw[:104, :]
            ar = area[:, cols(q)]
            wts = jnp.concatenate([va, va], axis=1) * jnp.concatenate([ar, ar], axis=1)
            d = a - jnp.concatenate([tg, tg], axis=1)
            g = wts * (smooth_sign(d) * (1.0 / members) - pair_coef * pairs)
            gp[q] = jnp.concatenate([g, jnp.zeros((24, 2 * CQ), f32)], axis=0).astype(bf16)

        def back_pre(q):
            gs[:104, :] += dot_nt(gp[q], act[q])[:104]
            for o in range(4):
                rows = pl.ds(o * 256, 256)
                g = (dot(wot[rows, :], gp[q]) * slope[q, rows, :]).astype(bf16)
                act[q, rows, :] = g
                gf = g.astype(f32)
                bacc[rows, :] += gf[:, :128] + gf[:, 128:]

        def back_w(q, o):
            rows = pl.ds(o * 256, 256)
            gw[rows, :] += dot_nt(act[q, rows, :], hid[q])

        def late(j):
            if j < 4:
                for i in range(4):
                    hid[i, pl.ds(j * 256, 256), :] = w[i * 256:(i + 1) * 256, j * 256:(j + 1) * 256].T
            else:
                q = (j - 4) // 2
                rows = pl.ds((j - 4) % 2 * 512, 512)
                g = sum(dot(hid[i, rows, :], act[q, i * 256:(i + 1) * 256, :]) for i in range(4)).astype(bf16)
                for i in range(2):
                    ghs[i, rows, pl.ds(q * CQ, CQ)] = g[:, i * CQ:(i + 1) * CQ]

        gw[...] = jnp.zeros((1024, 1024), f32)
        bacc[...] = jnp.zeros((1024, 128), f32)
        for cp in small_in[:5]:
            cp.wait()
        bcol[...] = jnp.broadcast_to(brow[...], (128, 1024)).T
        vw[...] = jnp.zeros((128, 128), f32)
        vw[:, :100] = jnp.broadcast_to(vwrow[...], (128, 100))
        vw[...] = vw[...].T
        tgt[96:104, :] = jnp.zeros((8, 1024), f32)
        tgt[:100, :] = tgt_in[...]
        gs[...] = jnp.zeros((128, 1024), f32)
        gs[:100, :] = wo_in[...].astype(f32)
        wo[...] = gs[...].astype(bf16)
        wot[...] = gs[...].T.astype(bf16)
        gs[...] = jnp.zeros((128, 1024), f32)
        small_in[5].wait()

        def fwd_step(q, _):
            forward(q)
            @pl.when(q == 0)
            def _():
                pl.semaphore_wait(bar, len(peers))
            cp_x(q).start()
            cp_p(q).start()
            return 0
        lax.fori_loop(0, NQ, fwd_step, 0)

        def hand_on(q):
            cp_x(q).wait_recv()
            cp_f(q).start()
        def arrive(q):
            cp_p(q).wait_recv()
            cp_f(q).wait_recv()
            grad_pred(q)
            back_pre(q)
        def bwd_step(q, _):
            arrive(q)
            hand_on(q + 1)
            for o in range(4):
                back_w(q, o)
            return 0
        hand_on(0)
        lax.fori_loop(0, NQ - 1, bwd_step, 0)
        last = NQ - 1
        arrive(last)
        back_w(last, 0)
        core_send(1)
        ones = jnp.ones((8, 128), f32)
        gs[104:112, :] = lax.dot_general(ones, bacc[...], NT, precision=lax.Precision.HIGHEST, preferred_element_type=f32)
        core_send(0)
        for k in range(2, n):
            back_w(last, k - 1)
            core_send(k)
        def st_out(k):
            pend["ac", k].wait_recv()
        steps = {0: st_core, 1: st_1, 2: st_2, 3: st_z, 4: st_ag2, 5: st_ag1, 6: st_agc, 7: st_out}
        for stage, k in ORDER:
            if stage == 9:
                late(k)
            else:
                steps[stage](k)
        for cp in sends:
            cp.wait_send()
        def finish(q, _):
            cp_x(q).wait_send()
            cp_p(q).wait_send()
            cp_f(q).wait_send()
            return 0
        lax.fori_loop(0, NQ, finish, 0)

    V = pltpu.VMEM
    D = pltpu.SemaphoreType.DMA
    W2 = 2 * CQ
    scratch = [V((1024, 1024), bf16), V((1, 1024), f32), V((100, 1024), bf16), V((100, 1024), f32), V((1, 1024), f32), V((1, 100), f32),
               V((NQ, 1024, W2), bf16), V((128, 1024), bf16), V((1024, 128), bf16),
               V((1024, 128), f32), V((128, 128), f32), V((104, 1024), f32),
               V((NQ, 1024, W2), bf16), V((NQ, 1024, W2), f32),
               V((NQ, 104, W2), f32), V((NQ, 104, W2), f32), V((NQ, 104, W2), f32), V((NQ, 104, W2), f32),
               V((NQ, 128, W2), bf16), V((1024, 128), f32), V((1024, 1024), f32), V((128, 1024), f32)]
    scratch += [V((NC, half, 1024), f32), V((128, 512), f32), V((128, 512), f32),
               V((NC, 2, 3, 4 * pr, 512), f32), V((2, 3, 32, 256), f32), V((NC, 2, 4 * pr, 512), f32), V((2, 32, 256), f32),
               V((NC, 2, 3, pr, 512), f32), V((2, 3, 8, 256), f32), V((NC, pr, 1024), f32), V((8, 512), f32),
               V((NC, 7, pr, 128), f32), V((7, 8, 512), f32)]
    scratch += [D((NQ, 2)), D((6,))] + [D((NQ,))] * 6
    for shp in ((n,), (n, 2, 3), (n, 2, 3), (n, 7), (n, 7), (n, 2, 3), (n, 2, 3), (n,)):
        scratch += [D(shp), D(shp)]
    vm = pl.BlockSpec(memory_space=pltpu.VMEM)
    hbm = pl.BlockSpec(memory_space=pl.ANY)
    return pl.pallas_call(kern,
        out_shape=(jax.ShapeDtypeStruct((2, 1024, 1024), bf16), jax.ShapeDtypeStruct((1024, 1024), f32), jax.ShapeDtypeStruct((128, 1024), f32)),
        in_specs=[pl.BlockSpec(memory_space=pltpu.HBM)] * 7, out_specs=[vm, vm, vm],
        scratch_shapes=scratch, name="fused",
        compiler_params=pltpu.CompilerParams(collective_id=3, has_side_effects=True, vmem_limit_bytes=44 * 2**20))


def place(ghs, ow, os):
    def kern(ghs, ow, os, gh, gw, go, gb, out, sem):
        out[...] = os[:100, :]
        cps = [pltpu.make_async_copy(ow, gw, sem.at[0]), pltpu.make_async_copy(out, go, sem.at[1]), pltpu.make_async_copy(ghs, gh, sem.at[2])]
        for cp in cps:
            cp.start()
        gb[...] = os[104:105, :]
        for cp in cps:
            cp.wait()
    vm = pl.BlockSpec(memory_space=pltpu.VMEM)
    hbm = pl.BlockSpec(memory_space=pl.ANY)
    return pl.pallas_call(kern, out_shape=(jax.ShapeDtypeStruct((2, 1024, 1024), bf16), jax.ShapeDtypeStruct((1024, 1024), f32),
                                           jax.ShapeDtypeStruct((100, 1024), f32), jax.ShapeDtypeStruct((1, 1024), f32)),
        in_specs=[vm, vm, vm], out_specs=[hbm, hbm, hbm, vm], scratch_shapes=[pltpu.VMEM((100, 1024), f32), pltpu.SemaphoreType.DMA((3,))], name="place",
        compiler_params=pltpu.CompilerParams(has_side_effects=True, vmem_limit_bytes=2**20))(ghs, ow, os)


def per_device(hidden, w_first, b_first, w_out, target, area, var_weight):
    members = hidden.shape[0] * lax.axis_size("mem")
    total = members * hidden.shape[2] * lax.axis_size("pts")
    scale = 1.0 / math.sqrt(total)
    eps_fair = 0.05 / members
    pair_coef = (1.0 - eps_fair) / (members * (members - 1))
    args = [pltpu.with_memory_space_constraint(a, pltpu.HBM) for a in (hidden, w_first, b_first[None], w_out, target, area[None], var_weight[None])]
    ghs, ow, os = make_kernel(members, pair_coef, scale)(*args)
    grad_hidden, grad_first, grad_out, grad_bias = place(ghs, ow, os)
    return (grad_hidden, grad_first, grad_out, grad_bias[0])


def solution(mesh):
    return jax.shard_map(
        per_device,
        mesh=mesh,
        in_specs=(P("mem", None, "pts"), P(), P(), P(), P(None, "pts"), P("pts"), P()),
        out_specs=(P("mem", None, "pts"), P(), P(), P()),
        check_vma=False,
    )
```

```python
import math

import jax
import jax.numpy as jnp
from jax import lax
from jax.experimental import pallas as pl
from jax.experimental.pallas import tpu as pltpu
from jax.sharding import PartitionSpec as P

MESH = pl.DeviceIdType.MESH
f32 = jnp.float32
bf16 = jnp.bfloat16
curve = 0.044715
root_coef = 0.7978845608
delta_sq = 0.0025
NQ = 8
CQ = 128
NC = 4
NT = (((1,), (1,)), ((), ()))
ORDER = (
    (0, 1), (0, 0), (0, 2), (1, 1), (9, 0), (9, 1), (9, 2), (9, 3), (0, 3), (1, 2), (2, 1), (1, 0), (9, 4), (9, 5),
    (9, 6), (9, 7), (0, 4), (1, 3), (2, 2), (3, 1), (2, 0), (9, 8), (9, 9), (9, 10), (9, 11), (1, 4), (2, 3), (3, 2),
    (4, 1), (9, 12), (9, 13), (9, 14), (9, 15), (2, 4), (3, 3), (4, 2), (5, 1), (3, 0), (9, 16), (9, 17), (9, 18),
    (9, 19), (3, 4), (4, 3), (5, 2), (6, 1), (4, 0), (4, 4), (5, 3), (6, 2), (7, 1), (5, 0), (5, 4), (6, 3), (7, 2),
    (6, 4), (7, 3), (6, 0), (7, 4),
)


def smooth_sign(d):
    return d * lax.rsqrt(d * d + delta_sq)


def dot(a, b):
    return jnp.dot(a, b, preferred_element_type=f32)


def dot_nt(a, b):
    return lax.dot_general(a, b, NT, preferred_element_type=f32)


def make_kernel(members, pair_coef, scale):
    pr = 32 // NC
    half = 16 * pr
    n = NC + 1

    def kern(hid_hbm, w_hbm, b_hbm, wo_hbm, tgt_hbm, area_hbm, vw_hbm, ghs, ow, os,
             w, brow, wo_in, tgt_in, area, vwrow, hid, wo, wot, bcol, vw, tgt, act, slope, pred, pc, px, py, gp, bacc, gw, gs,
             rcw, rcs, as_, r1w, b1w, r2w, zw, rzw, rzs, zs, rxs, rys,
             q_h, q_in, s_x, q_x, s_p, q_p, s_f, q_f,
             s_c, q_c, s_1, q_1, s_2, q_2, s_z, q_z, s_az, q_az, s_a2, q_a2, s_a1, q_a1, s_ac, q_ac,
             s_sz, q_sz, s_sx, q_sx, s_sy, q_sy, s_tx, q_tx, s_tz, q_tz):
        m = lax.axis_index("mem"); p = lax.axis_index("pts")
        c = m % 2
        x = (m // 2) * 2 + p % 2
        y = (p // 2) % 4
        z = p // 8
        def at(xx, yy, zz, cc):
            return ((xx // 2) * 2 + cc, (zz * 4 + yy) * 2 + xx % 2)
        def xo(d): return at((x + d) % 4, y, z, c)
        def yo(d): return at(x, (y + d) % 4, z, c)
        def zo(d): return at(x, y, (z + d) % 8, c)
        other = at(x, y, z, 1 - c)
        def mo(v, k): return pl.multiple_of(v, k)
        def cols(q): return pl.ds(mo(q * CQ, CQ), CQ)

        def load(q, i):
            return pltpu.make_async_copy(hid_hbm.at[i, :, cols(q)], hid.at[q, :, pl.ds(i * CQ, CQ)], q_h.at[q, i])
        small_in = [pltpu.make_async_copy(a, b, q_in.at[i]) for i, (a, b) in enumerate(
            ((b_hbm, brow), (vw_hbm, vwrow), (wo_hbm, wo_in), (tgt_hbm, tgt_in), (area_hbm, area), (w_hbm, w)))]
        for cp in small_in:
            cp.start()
        for q in range(NQ):
            for i in range(2):
                load(q, i).start()

        bar = pltpu.get_barrier_semaphore()
        peers = [other] + [xo(d) for d in (1, 2, 3)] + [yo(d) for d in (1, 2, 3)] + [zo(d) for d in range(1, 8)]
        for t in peers:
            pl.semaphore_signal(bar, inc=1, device_id=t, device_id_type=MESH)

        def remote(src, dst, ss, rs, dev):
            return pltpu.make_async_remote_copy(src_ref=src, dst_ref=dst, send_sem=ss, recv_sem=rs, device_id=dev, device_id_type=MESH)
        def cp_x(q): return remote(pred.at[q], px.at[q], s_x.at[q], q_x.at[q], xo(2))
        def cp_p(q): return remote(pred.at[q], pc.at[q], s_p.at[q], q_p.at[q], other)
        def cp_f(q): return remote(px.at[q], py.at[q], s_f.at[q], q_f.at[q], other)

        sends = []
        def copy(src, dst, ss, rs, dev):
            cp = remote(src, dst, ss, rs, dev)
            cp.start(); sends.append(cp); return cp
        pend = {}
        def small_cols(j, w): return pl.ds(mo(c * 512 + j * w, w), w)
        def mine(k): return gw.at[pl.ds(mo((k - 1) * 2 * half + c * half, half), half)]
        def done(k): return ow.at[pl.ds(mo((k - 1) * 2 * half + c * half, half), half)]
        def axis(h): return ((x, xo), (y, yo))[h]

        def core_send(k):
            if k == 0:
                src, dst = gs.at[:, pl.ds(mo((1 - c) * 512, 512), 512)], rcs
            else:
                src, dst = gw.at[pl.ds(mo((k - 1) * 2 * half + (1 - c) * half, half), half)], rcw.at[k - 1]
            pend["c", k] = copy(src, dst, s_c.at[k], q_c.at[k], other)

        def small_0():
            pend["c", 0].wait_recv()
            as_[...] = gs[:, pl.ds(mo(c * 512, 512), 512)] + rcs[...]
            for d in (4, 3, 5, 2, 6, 1, 7):
                t = (z + d) % 8
                pend["sz", d] = copy(as_.at[pl.ds(mo(t * 16, 16), 16)], rzs.at[d - 1], s_sz.at[d - 1], q_sz.at[d - 1], zo(d))
        def small_1():
            for d in range(1, 8):
                pend["sz", d].wait_recv()
            tot = as_[pl.ds(mo(z * 16, 16), 16), :]
            for d in range(7):
                tot = tot + rzs[d]
            zs[...] = tot
            for d in (2, 1, 3):
                t = (x + d) % 4
                pend["sx", d] = copy(zs.at[:, pl.ds(mo(t * 128, 128), 128)], rxs.at[d - 1], s_sx.at[d - 1], q_sx.at[d - 1], xo(d))
        def small_2():
            for d in range(1, 4):
                pend["sx", d].wait_recv()
            rys[y] = zs[:, pl.ds(mo(x * 128, 128), 128)] + rxs[0] + rxs[1] + rxs[2]
            for d in (2, 1, 3):
                pend["sy", d] = copy(rys.at[y], rys.at[y], s_sy.at[d - 1], q_sy.at[d - 1], yo(d))
        def small_3():
            for d in range(1, 4):
                pend["sy", d].wait_recv()
            blk = os.at[pl.ds(mo(z * 16, 16), 16), small_cols(x, 128)]
            blk[...] = ((rys[0] + rys[1]) + (rys[2] + rys[3])) * scale
            for d in (2, 1, 3):
                pend["tx", d] = copy(blk, blk, s_tx.at[d - 1], q_tx.at[d - 1], xo(d))
        def small_4():
            for d in range(1, 4):
                pend["tx", d].wait_recv()
            blk = os.at[pl.ds(mo(z * 16, 16), 16), small_cols(0, 512)]
            for d in (4, 3, 5, 2, 6, 1, 7):
                pend["tz", d] = copy(blk, blk, s_tz.at[d - 1], q_tz.at[d - 1], zo(d))
        def small_5():
            for d in range(1, 8):
                pend["tz", d].wait_recv()
            blk = os.at[:, small_cols(0, 512)]
            pend["ac", 0] = copy(blk, blk, s_ac.at[0], q_ac.at[0], other)

        def st_core(k):
            pend["c", k].wait_recv()
            a = mine(k)
            a[...] += rcw[k - 1]
            for d in (2, 1, 3):
                for h in (0, 1):
                    me, to = axis(h)
                    t = (me + d) % 4
                    pend[1, k, h, d] = copy(a.at[pl.ds(mo(t * 4 * pr, 4 * pr), 4 * pr), pl.ds(h * 512, 512)], r1w.at[k - 1, h, d - 1], s_1.at[k, h, d - 1], q_1.at[k, h, d - 1], to(d))
        def st_1(k):
            for h in (0, 1):
                me, to = axis(h)
                nxt, along = axis(1 - h)
                for d in (1, 2, 3):
                    pend[1, k, h, d].wait_recv()
                b1w[k - 1, h] = mine(k)[pl.ds(mo(me * 4 * pr, 4 * pr), 4 * pr), pl.ds(h * 512, 512)] + r1w[k - 1, h, 0] + r1w[k - 1, h, 1] + r1w[k - 1, h, 2]
                for d in (2, 1, 3):
                    t = (nxt + d) % 4
                    pend[2, k, h, d] = copy(b1w.at[k - 1, h, pl.ds(mo(t * pr, pr), pr)], r2w.at[k - 1, h, d - 1], s_2.at[k, h, d - 1], q_2.at[k, h, d - 1], along(d))
        def st_2(k):
            for h in (0, 1):
                nxt, along = axis(1 - h)
                for d in (1, 2, 3):
                    pend[2, k, h, d].wait_recv()
                zw[k - 1, :, pl.ds(h * 512, 512)] = b1w[k - 1, h, pl.ds(mo(nxt * pr, pr), pr)] + r2w[k - 1, h, 0] + r2w[k - 1, h, 1] + r2w[k - 1, h, 2]
            for d in (4, 3, 5, 2, 6, 1, 7):
                t = (z + d) % 8
                pend["z", k, d] = copy(zw.at[k - 1, :, pl.ds(mo(t * 128, 128), 128)], rzw.at[k - 1, d - 1], s_z.at[k, d - 1], q_z.at[k, d - 1], zo(d))
        def st_z(k):
            for d in range(1, 8):
                pend["z", k, d].wait_recv()
            tot = zw[k - 1, :, pl.ds(mo(z * 128, 128), 128)]
            for d in range(7):
                tot = tot + rzw[k - 1, d]
            hz = z // 4
            j = (1 - hz) * (4 * x + y) + hz * (4 * y + x)
            dst = done(k).at[pl.ds(mo(j * pr, pr), pr), pl.ds(mo(z * 128, 128), 128)]
            dst[...] = tot * scale
            for d in (4, 3, 5, 2, 6, 1, 7):
                pend["az", k, d] = copy(dst, dst, s_az.at[k, d - 1], q_az.at[k, d - 1], zo(d))
        def st_ag2(k):
            for d in range(1, 8):
                pend["az", k, d].wait_recv()
            for h in (0, 1):
                me, to = axis(h)
                nxt, along = axis(1 - h)
                blk = done(k).at[pl.ds(mo((4 * me + nxt) * pr, pr), pr), pl.ds(h * 512, 512)]
                for d in (2, 1, 3):
                    pend["a2", k, h, d] = copy(blk, blk, s_a2.at[k, h, d - 1], q_a2.at[k, h, d - 1], along(d))
        def st_ag1(k):
            for h in (0, 1):
                me, to = axis(h)
                for d in (1, 2, 3):
                    pend["a2", k, h, d].wait_recv()
                blk = done(k).at[pl.ds(mo(me * 4 * pr, 4 * pr), 4 * pr), pl.ds(h * 512, 512)]
                for d in (2, 1, 3):
                    pend["a1", k, h, d] = copy(blk, blk, s_a1.at[k, h, d - 1], q_a1.at[k, h, d - 1], to(d))
        def st_agc(k):
            for h in (0, 1):
                for d in (1, 2, 3):
                    pend["a1", k, h, d].wait_recv()
            blk = done(k)
            pend["ac", k] = copy(blk, blk, s_ac.at[k], q_ac.at[k], other)

        def forward(q):
            for i in range(2):
                load(q, i).wait()
            for o in range(4):
                rows = pl.ds(o * 256, 256)
                bias = bcol[rows, :]
                u = dot(w[rows, :], hid[q]) + jnp.concatenate([bias, bias], axis=1)
                u2 = u * u
                t = jnp.tanh(u * (root_coef + root_coef * curve * u2))
                h = 0.5 + 0.5 * t
                a = u * h
                act[q, rows, :] = a.astype(bf16)
                slope[q, rows, :] = h + (a - a * h) * (2.0 * root_coef + 6.0 * root_coef * curve * u2)
            pred[q] = dot(wo[...], act[q])[:104]

        def grad_pred(q):
            a = pred[q]
            s01 = smooth_sign(a[:, :CQ] - a[:, CQ:])
            pairs = jnp.concatenate([s01, -s01], axis=1)
            for ref in (pc, px, py):
                v = ref[q]
                sw = jnp.concatenate([v[:, CQ:], v[:, :CQ]], axis=1)
                pairs = pairs + (smooth_sign(a - v) + smooth_sign(a - sw))
            tg = tgt[:, cols(q)]
            va = vw[:104, :]
            ar = area[:, cols(q)]
            wts = jnp.concatenate([va, va], axis=1) * jnp.concatenate([ar, ar], axis=1)
            d = a - jnp.concatenate([tg, tg], axis=1)
            g = wts * (smooth_sign(d) * (1.0 / members) - pair_coef * pairs)
            gp[q] = jnp.concatenate([g, jnp.zeros((24, 2 * CQ), f32)], axis=0).astype(bf16)

        def back_pre(q):
            gs[:104, :] += dot_nt(gp[q], act[q])[:104]
            for o in range(4):
                rows = pl.ds(o * 256, 256)
                g = (dot(wot[rows, :], gp[q]) * slope[q, rows, :]).astype(bf16)
                act[q, rows, :] = g
                gf = g.astype(f32)
                bacc[rows, :] += gf[:, :128] + gf[:, 128:]

        def back_w(q, o):
            rows = pl.ds(o * 256, 256)
            gw[rows, :] += dot_nt(act[q, rows, :], hid[q])

        def late(j):
            if j < 4:
                for i in range(4):
                    hid[i, pl.ds(j * 256, 256), :] = w[i * 256:(i + 1) * 256, j * 256:(j + 1) * 256].T
            else:
                q = (j - 4) // 2
                rows = pl.ds((j - 4) % 2 * 512, 512)
                g = sum(dot(hid[i, rows, :], act[q, i * 256:(i + 1) * 256, :]) for i in range(4)).astype(bf16)
                for i in range(2):
                    ghs[i, rows, pl.ds(q * CQ, CQ)] = g[:, i * CQ:(i + 1) * CQ]

        gw[...] = jnp.zeros((1024, 1024), f32)
        bacc[...] = jnp.zeros((1024, 128), f32)
        for cp in small_in[:5]:
            cp.wait()
        bcol[...] = jnp.broadcast_to(brow[...], (128, 1024)).T
        vw[...] = jnp.zeros((128, 128), f32)
        vw[:, :100] = jnp.broadcast_to(vwrow[...], (128, 100))
        vw[...] = vw[...].T
        tgt[96:104, :] = jnp.zeros((8, 1024), f32)
        tgt[:100, :] = tgt_in[...]
        gs[...] = jnp.zeros((128, 1024), f32)
        gs[:100, :] = wo_in[...].astype(f32)
        wo[...] = gs[...].astype(bf16)
        wot[...] = gs[...].T.astype(bf16)
        gs[...] = jnp.zeros((128, 1024), f32)
        small_in[5].wait()

        def fwd_step(q, _):
            forward(q)
            @pl.when(q == 0)
            def _():
                pl.semaphore_wait(bar, len(peers))
            cp_x(q).start()
            cp_p(q).start()
            return 0
        lax.fori_loop(0, NQ, fwd_step, 0)

        def hand_on(q):
            cp_x(q).wait_recv()
            cp_f(q).start()
        def arrive(q):
            cp_p(q).wait_recv()
            cp_f(q).wait_recv()
            grad_pred(q)
            back_pre(q)
        def bwd_step(q, _):
            arrive(q)
            hand_on(q + 1)
            for o in range(4):
                back_w(q, o)
            return 0
        hand_on(0)
        lax.fori_loop(0, NQ - 1, bwd_step, 0)
        last = NQ - 1
        arrive(last)
        back_w(last, 0)
        core_send(1)
        for k in range(2, n):
            back_w(last, k - 1)
            core_send(k)
        ones = jnp.ones((8, 128), f32)
        gs[104:112, :] = lax.dot_general(ones, bacc[...], NT, precision=lax.Precision.HIGHEST, preferred_element_type=f32)
        core_send(0)
        def st_out(k):
            pend["ac", k].wait_recv()
        big = (st_core, st_1, st_2, st_z, st_ag2, st_ag1, st_agc, st_out)
        small = (small_0, small_1, small_2, small_3, small_4, small_5, lambda: st_out(0))
        for stage, k in ORDER:
            if stage == 9:
                late(k)
            else:
                if k == 0:
                    small[stage]()
                else:
                    big[stage](k)
        for cp in sends:
            cp.wait_send()
        def finish(q, _):
            cp_x(q).wait_send()
            cp_p(q).wait_send()
            cp_f(q).wait_send()
            return 0
        lax.fori_loop(0, NQ, finish, 0)

    V = pltpu.VMEM
    D = pltpu.SemaphoreType.DMA
    W2 = 2 * CQ
    scratch = [V((1024, 1024), bf16), V((1, 1024), f32), V((100, 1024), bf16), V((100, 1024), f32), V((1, 1024), f32), V((1, 100), f32),
               V((NQ, 1024, W2), bf16), V((128, 1024), bf16), V((1024, 128), bf16),
               V((1024, 128), f32), V((128, 128), f32), V((104, 1024), f32),
               V((NQ, 1024, W2), bf16), V((NQ, 1024, W2), f32),
               V((NQ, 104, W2), f32), V((NQ, 104, W2), f32), V((NQ, 104, W2), f32), V((NQ, 104, W2), f32),
               V((NQ, 128, W2), bf16), V((1024, 128), f32), V((1024, 1024), f32), V((128, 1024), f32)]
    scratch += [V((NC, half, 1024), f32), V((128, 512), f32), V((128, 512), f32),
                V((NC, 2, 3, 4 * pr, 512), f32), V((NC, 2, 4 * pr, 512), f32), V((NC, 2, 3, pr, 512), f32),
                V((NC, pr, 1024), f32), V((NC, 7, pr, 128), f32),
                V((7, 16, 512), f32), V((16, 512), f32), V((3, 16, 128), f32), V((4, 16, 128), f32)]
    scratch += [D((NQ, 2)), D((6,))] + [D((NQ,))] * 6
    for shp in ((n,), (n, 2, 3), (n, 2, 3), (n, 7), (n, 7), (n, 2, 3), (n, 2, 3), (n,), (7,), (3,), (3,), (3,), (7,)):
        scratch += [D(shp), D(shp)]
    vm = pl.BlockSpec(memory_space=pltpu.VMEM)
    hbm = pl.BlockSpec(memory_space=pl.ANY)
    return pl.pallas_call(kern,
        out_shape=(jax.ShapeDtypeStruct((2, 1024, 1024), bf16), jax.ShapeDtypeStruct((1024, 1024), f32), jax.ShapeDtypeStruct((128, 1024), f32)),
        in_specs=[pl.BlockSpec(memory_space=pltpu.HBM)] * 7, out_specs=[vm, vm, vm],
        scratch_shapes=scratch, name="fused",
        compiler_params=pltpu.CompilerParams(collective_id=3, has_side_effects=True, vmem_limit_bytes=44 * 2**20))


def place(ghs, ow, os):
    def kern(ghs, ow, os, gh, gw, go, gb, out, sem):
        out[...] = os[:100, :]
        cps = [pltpu.make_async_copy(ow, gw, sem.at[0]), pltpu.make_async_copy(out, go, sem.at[1]), pltpu.make_async_copy(ghs, gh, sem.at[2])]
        for cp in cps:
            cp.start()
        gb[...] = os[104:105, :]
        for cp in cps:
            cp.wait()
    vm = pl.BlockSpec(memory_space=pltpu.VMEM)
    hbm = pl.BlockSpec(memory_space=pl.ANY)
    return pl.pallas_call(kern, out_shape=(jax.ShapeDtypeStruct((2, 1024, 1024), bf16), jax.ShapeDtypeStruct((1024, 1024), f32),
                                           jax.ShapeDtypeStruct((100, 1024), f32), jax.ShapeDtypeStruct((1, 1024), f32)),
        in_specs=[vm, vm, vm], out_specs=[hbm, hbm, hbm, vm], scratch_shapes=[pltpu.VMEM((100, 1024), f32), pltpu.SemaphoreType.DMA((3,))], name="place",
        compiler_params=pltpu.CompilerParams(has_side_effects=True, vmem_limit_bytes=2**20))(ghs, ow, os)


def per_device(hidden, w_first, b_first, w_out, target, area, var_weight):
    members = hidden.shape[0] * lax.axis_size("mem")
    total = members * hidden.shape[2] * lax.axis_size("pts")
    scale = 1.0 / math.sqrt(total)
    eps_fair = 0.05 / members
    pair_coef = (1.0 - eps_fair) / (members * (members - 1))
    args = [pltpu.with_memory_space_constraint(a, pltpu.HBM) for a in (hidden, w_first, b_first[None], w_out, target, area[None], var_weight[None])]
    ghs, ow, os = make_kernel(members, pair_coef, scale)(*args)
    grad_hidden, grad_first, grad_out, grad_bias = place(ghs, ow, os)
    return (grad_hidden, grad_first, grad_out, grad_bias[0])


def solution(mesh):
    return jax.shard_map(
        per_device,
        mesh=mesh,
        in_specs=(P("mem", None, "pts"), P(), P(), P(), P(None, "pts"), P("pts"), P()),
        out_specs=(P("mem", None, "pts"), P(), P(), P()),
        check_vma=False,
    )
```

```python
import math

import jax
import jax.numpy as jnp
from jax import lax
from jax.experimental import pallas as pl
from jax.experimental.pallas import tpu as pltpu
from jax.sharding import PartitionSpec as P

MESH = pl.DeviceIdType.MESH
f32 = jnp.float32
bf16 = jnp.bfloat16
curve = 0.044715
root_coef = 0.7978845608
delta_sq = 0.0025
NQ = 8
CQ = 128
NC = 4
NT = (((1,), (1,)), ((), ()))
ORDER = (
    (0, 1), (0, 0), (0, 2), (1, 1), (9, 0), (9, 1), (9, 2), (9, 3), (0, 3), (1, 2), (2, 1), (1, 0), (9, 4), (9, 5),
    (9, 6), (9, 7), (0, 4), (1, 3), (2, 2), (3, 1), (2, 0), (9, 8), (9, 9), (9, 10), (9, 11), (1, 4), (2, 3), (3, 2),
    (4, 1), (9, 12), (9, 13), (9, 14), (9, 15), (2, 4), (3, 3), (4, 2), (5, 1), (3, 0), (9, 16), (9, 17), (9, 18),
    (9, 19), (3, 4), (4, 3), (5, 2), (6, 1), (4, 0), (4, 4), (5, 3), (6, 2), (7, 1), (5, 0), (5, 4), (6, 3), (7, 2),
    (6, 4), (7, 3), (6, 0), (7, 4),
)


def smooth_sign(d):
    return d * lax.rsqrt(d * d + delta_sq)


def dot(a, b):
    return jnp.dot(a, b, preferred_element_type=f32)


def dot_nt(a, b):
    return lax.dot_general(a, b, NT, preferred_element_type=f32)


def make_kernel(members, pair_coef, scale):
    pr = 32 // NC
    half = 16 * pr
    n = NC + 1

    def kern(hid_hbm, w_hbm, b_hbm, wo_hbm, tgt_hbm, area_hbm, vw_hbm, ghs, ow, os,
             w, brow, wo_in, tgt_in, area, vwrow, glast, hid, wo, wot, bcol, vw, tgt, act, slope, pred, pc, px, py, gp, bacc, gw, gs,
             rcw, rcs, as_, r1w, b1w, r2w, zw, rzw, rzs, zs, rxs, rys,
             q_h, q_in, s_x, q_x, s_p, q_p, s_f, q_f,
             s_c, q_c, s_1, q_1, s_2, q_2, s_z, q_z, s_az, q_az, s_a2, q_a2, s_a1, q_a1, s_ac, q_ac,
             s_sz, q_sz, s_sx, q_sx, s_sy, q_sy, s_tx, q_tx, s_tz, q_tz):
        m = lax.axis_index("mem"); p = lax.axis_index("pts")
        c = m % 2
        x = (m // 2) * 2 + p % 2
        y = (p // 2) % 4
        z = p // 8
        def at(xx, yy, zz, cc):
            return ((xx // 2) * 2 + cc, (zz * 4 + yy) * 2 + xx % 2)
        def xo(d): return at((x + d) % 4, y, z, c)
        def yo(d): return at(x, (y + d) % 4, z, c)
        def zo(d): return at(x, y, (z + d) % 8, c)
        other = at(x, y, z, 1 - c)
        def mo(v, k): return pl.multiple_of(v, k)
        def cols(q): return pl.ds(mo(q * CQ, CQ), CQ)

        def load(q, i):
            return pltpu.make_async_copy(hid_hbm.at[i, :, cols(q)], hid.at[q, :, pl.ds(i * CQ, CQ)], q_h.at[q, i])
        small_in = [pltpu.make_async_copy(a, b, q_in.at[i]) for i, (a, b) in enumerate(
            ((b_hbm, brow), (vw_hbm, vwrow), (wo_hbm, wo_in), (tgt_hbm, tgt_in), (area_hbm, area), (w_hbm, w)))]
        for cp in small_in:
            cp.start()
        for q in range(NQ):
            for i in range(2):
                load(q, i).start()

        bar = pltpu.get_barrier_semaphore()
        peers = [other] + [xo(d) for d in (1, 2, 3)] + [yo(d) for d in (1, 2, 3)] + [zo(d) for d in range(1, 8)]
        for t in peers:
            pl.semaphore_signal(bar, inc=1, device_id=t, device_id_type=MESH)

        def remote(src, dst, ss, rs, dev):
            return pltpu.make_async_remote_copy(src_ref=src, dst_ref=dst, send_sem=ss, recv_sem=rs, device_id=dev, device_id_type=MESH)
        def cp_x(q): return remote(pred.at[q], px.at[q], s_x.at[q], q_x.at[q], xo(2))
        def cp_p(q): return remote(pred.at[q], pc.at[q], s_p.at[q], q_p.at[q], other)
        def cp_f(q): return remote(px.at[q], py.at[q], s_f.at[q], q_f.at[q], other)

        sends = []
        def copy(src, dst, ss, rs, dev):
            cp = remote(src, dst, ss, rs, dev)
            cp.start(); sends.append(cp); return cp
        pend = {}
        def small_cols(j, w): return pl.ds(mo(c * 512 + j * w, w), w)
        def mine(k): return gw.at[pl.ds(mo((k - 1) * 2 * half + c * half, half), half)]
        def done(k): return ow.at[pl.ds(mo((k - 1) * 2 * half + c * half, half), half)]
        def axis(h): return ((x, xo), (y, yo))[h]

        def core_send(k):
            if k == 0:
                src, dst = gs.at[:, pl.ds(mo((1 - c) * 512, 512), 512)], rcs
            else:
                src, dst = gw.at[pl.ds(mo((k - 1) * 2 * half + (1 - c) * half, half), half)], rcw.at[k - 1]
            pend["c", k] = copy(src, dst, s_c.at[k], q_c.at[k], other)

        def small_0():
            pend["c", 0].wait_recv()
            as_[...] = gs[:, pl.ds(mo(c * 512, 512), 512)] + rcs[...]
            for d in (4, 3, 5, 2, 6, 1, 7):
                t = (z + d) % 8
                pend["sz", d] = copy(as_.at[pl.ds(mo(t * 16, 16), 16)], rzs.at[d - 1], s_sz.at[d - 1], q_sz.at[d - 1], zo(d))
        def small_1():
            for d in range(1, 8):
                pend["sz", d].wait_recv()
            tot = as_[pl.ds(mo(z * 16, 16), 16), :]
            for d in range(7):
                tot = tot + rzs[d]
            zs[...] = tot
            for d in (2, 1, 3):
                t = (x + d) % 4
                pend["sx", d] = copy(zs.at[:, pl.ds(mo(t * 128, 128), 128)], rxs.at[d - 1], s_sx.at[d - 1], q_sx.at[d - 1], xo(d))
        def small_2():
            for d in range(1, 4):
                pend["sx", d].wait_recv()
            rys[y] = zs[:, pl.ds(mo(x * 128, 128), 128)] + rxs[0] + rxs[1] + rxs[2]
            for d in (2, 1, 3):
                pend["sy", d] = copy(rys.at[y], rys.at[y], s_sy.at[d - 1], q_sy.at[d - 1], yo(d))
        def small_3():
            for d in range(1, 4):
                pend["sy", d].wait_recv()
            blk = os.at[pl.ds(mo(z * 16, 16), 16), small_cols(x, 128)]
            blk[...] = ((rys[0] + rys[1]) + (rys[2] + rys[3])) * scale
            for d in (2, 1, 3):
                pend["tx", d] = copy(blk, blk, s_tx.at[d - 1], q_tx.at[d - 1], xo(d))
        def small_4():
            for d in range(1, 4):
                pend["tx", d].wait_recv()
            blk = os.at[pl.ds(mo(z * 16, 16), 16), small_cols(0, 512)]
            for d in (4, 3, 5, 2, 6, 1, 7):
                pend["tz", d] = copy(blk, blk, s_tz.at[d - 1], q_tz.at[d - 1], zo(d))
        def small_5():
            for d in range(1, 8):
                pend["tz", d].wait_recv()
            blk = os.at[:, small_cols(0, 512)]
            pend["ac", 0] = copy(blk, blk, s_ac.at[0], q_ac.at[0], other)

        def st_core(k):
            pend["c", k].wait_recv()
            a = mine(k)
            a[...] += rcw[k - 1]
            for d in (2, 1, 3):
                for h in (0, 1):
                    me, to = axis(h)
                    t = (me + d) % 4
                    pend[1, k, h, d] = copy(a.at[pl.ds(mo(t * 4 * pr, 4 * pr), 4 * pr), pl.ds(h * 512, 512)], r1w.at[k - 1, h, d - 1], s_1.at[k, h, d - 1], q_1.at[k, h, d - 1], to(d))
        def st_1(k):
            for h in (0, 1):
                me, to = axis(h)
                nxt, along = axis(1 - h)
                for d in (1, 2, 3):
                    pend[1, k, h, d].wait_recv()
                b1w[k - 1, h] = mine(k)[pl.ds(mo(me * 4 * pr, 4 * pr), 4 * pr), pl.ds(h * 512, 512)] + r1w[k - 1, h, 0] + r1w[k - 1, h, 1] + r1w[k - 1, h, 2]
                for d in (2, 1, 3):
                    t = (nxt + d) % 4
                    pend[2, k, h, d] = copy(b1w.at[k - 1, h, pl.ds(mo(t * pr, pr), pr)], r2w.at[k - 1, h, d - 1], s_2.at[k, h, d - 1], q_2.at[k, h, d - 1], along(d))
        def st_2(k):
            for h in (0, 1):
                nxt, along = axis(1 - h)
                for d in (1, 2, 3):
                    pend[2, k, h, d].wait_recv()
                zw[k - 1, :, pl.ds(h * 512, 512)] = b1w[k - 1, h, pl.ds(mo(nxt * pr, pr), pr)] + r2w[k - 1, h, 0] + r2w[k - 1, h, 1] + r2w[k - 1, h, 2]
            for d in (4, 3, 5, 2, 6, 1, 7):
                t = (z + d) % 8
                pend["z", k, d] = copy(zw.at[k - 1, :, pl.ds(mo(t * 128, 128), 128)], rzw.at[k - 1, d - 1], s_z.at[k, d - 1], q_z.at[k, d - 1], zo(d))
        def st_z(k):
            for d in range(1, 8):
                pend["z", k, d].wait_recv()
            tot = zw[k - 1, :, pl.ds(mo(z * 128, 128), 128)]
            for d in range(7):
                tot = tot + rzw[k - 1, d]
            hz = z // 4
            j = (1 - hz) * (4 * x + y) + hz * (4 * y + x)
            dst = done(k).at[pl.ds(mo(j * pr, pr), pr), pl.ds(mo(z * 128, 128), 128)]
            dst[...] = tot * scale
            for d in (4, 3, 5, 2, 6, 1, 7):
                pend["az", k, d] = copy(dst, dst, s_az.at[k, d - 1], q_az.at[k, d - 1], zo(d))
        def st_ag2(k):
            for d in range(1, 8):
                pend["az", k, d].wait_recv()
            for h in (0, 1):
                me, to = axis(h)
                nxt, along = axis(1 - h)
                blk = done(k).at[pl.ds(mo((4 * me + nxt) * pr, pr), pr), pl.ds(h * 512, 512)]
                for d in (2, 1, 3):
                    pend["a2", k, h, d] = copy(blk, blk, s_a2.at[k, h, d - 1], q_a2.at[k, h, d - 1], along(d))
        def st_ag1(k):
            for h in (0, 1):
                me, to = axis(h)
                for d in (1, 2, 3):
                    pend["a2", k, h, d].wait_recv()
                blk = done(k).at[pl.ds(mo(me * 4 * pr, 4 * pr), 4 * pr), pl.ds(h * 512, 512)]
                for d in (2, 1, 3):
                    pend["a1", k, h, d] = copy(blk, blk, s_a1.at[k, h, d - 1], q_a1.at[k, h, d - 1], to(d))
        def st_agc(k):
            for h in (0, 1):
                for d in (1, 2, 3):
                    pend["a1", k, h, d].wait_recv()
            blk = done(k)
            pend["ac", k] = copy(blk, blk, s_ac.at[k], q_ac.at[k], other)

        def forward(q):
            for i in range(2):
                load(q, i).wait()
            for o in range(4):
                rows = pl.ds(o * 256, 256)
                bias = bcol[rows, :]
                u = dot(w[rows, :], hid[q]) + jnp.concatenate([bias, bias], axis=1)
                u2 = u * u
                t = jnp.tanh(u * (root_coef + root_coef * curve * u2))
                h = 0.5 + 0.5 * t
                a = u * h
                act[q, rows, :] = a.astype(bf16)
                slope[q, rows, :] = h + (a - a * h) * (2.0 * root_coef + 6.0 * root_coef * curve * u2)
            pred[q] = dot(wo[...], act[q])[:104]

        def grad_pred(q):
            a = pred[q]
            s01 = smooth_sign(a[:, :CQ] - a[:, CQ:])
            pairs = jnp.concatenate([s01, -s01], axis=1)
            for ref in (pc, px, py):
                v = ref[q]
                sw = jnp.concatenate([v[:, CQ:], v[:, :CQ]], axis=1)
                pairs = pairs + (smooth_sign(a - v) + smooth_sign(a - sw))
            tg = tgt[:, cols(q)]
            va = vw[:104, :]
            ar = area[:, cols(q)]
            wts = jnp.concatenate([va, va], axis=1) * jnp.concatenate([ar, ar], axis=1)
            d = a - jnp.concatenate([tg, tg], axis=1)
            g = wts * (smooth_sign(d) * (1.0 / members) - pair_coef * pairs)
            gp[q] = jnp.concatenate([g, jnp.zeros((24, 2 * CQ), f32)], axis=0).astype(bf16)

        def pre_rows(q, rows):
            g = (dot(wot[rows, :], gp[q]) * slope[q, rows, :]).astype(bf16)
            gf = g.astype(f32)
            bacc[rows, :] += gf[:, :128] + gf[:, 128:]
            return g

        def back_pre(q):
            gs[:104, :] += dot_nt(gp[q], act[q])[:104]
            for o in range(4):
                rows = pl.ds(o * 256, 256)
                act[q, rows, :] = pre_rows(q, rows)

        def back_w(q, o):
            rows = pl.ds(o * 256, 256)
            gw[rows, :] += dot_nt(act[q, rows, :], hid[q])

        def late(j):
            if j < 4:
                for i in range(4):
                    hid[i, pl.ds(j * 256, 256), :] = w[i * 256:(i + 1) * 256, j * 256:(j + 1) * 256].T
            else:
                q = (j - 4) // 2
                rows = pl.ds((j - 4) % 2 * 512, 512)
                g = sum(dot(hid[i, rows, :], act[q, i * 256:(i + 1) * 256, :]) for i in range(4)).astype(bf16)
                for i in range(2):
                    ghs[i, rows, pl.ds(q * CQ, CQ)] = g[:, i * CQ:(i + 1) * CQ]

        small_in[0].wait()
        bcol[...] = jnp.broadcast_to(brow[...], (128, 1024)).T
        small_in[2].wait()
        gs[...] = jnp.zeros((128, 1024), f32)
        gs[:100, :] = wo_in[...].astype(f32)
        wo[...] = gs[...].astype(bf16)
        small_in[5].wait()

        def fwd_step(q, _):
            forward(q)
            @pl.when(q == 0)
            def _():
                pl.semaphore_wait(bar, len(peers))
            cp_x(q).start()
            cp_p(q).start()
            return 0
        lax.fori_loop(0, NQ, fwd_step, 0)

        def hand_on(q):
            cp_x(q).wait_recv()
            cp_f(q).start()
        hand_on(0)
        wot[...] = gs[...].T.astype(bf16)
        gs[...] = jnp.zeros((128, 1024), f32)
        gw[...] = jnp.zeros((1024, 1024), f32)
        bacc[...] = jnp.zeros((1024, 128), f32)
        for i in (1, 3, 4):
            small_in[i].wait()
        vw[...] = jnp.zeros((128, 128), f32)
        vw[:, :100] = jnp.broadcast_to(vwrow[...], (128, 100))
        vw[...] = vw[...].T
        tgt[96:104, :] = jnp.zeros((8, 1024), f32)
        tgt[:100, :] = tgt_in[...]

        def arrive(q):
            cp_p(q).wait_recv()
            cp_f(q).wait_recv()
            grad_pred(q)
        def bwd_step(q, _):
            arrive(q)
            back_pre(q)
            hand_on(q + 1)
            for o in range(4):
                back_w(q, o)
            return 0
        lax.fori_loop(0, NQ - 1, bwd_step, 0)
        last = NQ - 1
        arrive(last)
        for o in range(4):
            rows = pl.ds(o * 256, 256)
            glast[rows, :] = pre_rows(last, rows)
            gw[rows, :] += dot_nt(glast[rows, :], hid[last])
            core_send(o + 1)
        gs[:104, :] += dot_nt(gp[last], act[last])[:104]
        act[last] = glast[...]
        ones = jnp.ones((8, 128), f32)
        gs[104:112, :] = lax.dot_general(ones, bacc[...], NT, precision=lax.Precision.HIGHEST, preferred_element_type=f32)
        core_send(0)
        def st_out(k):
            pend["ac", k].wait_recv()
        big = (st_core, st_1, st_2, st_z, st_ag2, st_ag1, st_agc, st_out)
        small = (small_0, small_1, small_2, small_3, small_4, small_5, lambda: st_out(0))
        for stage, k in ORDER:
            if stage == 9:
                late(k)
            else:
                if k == 0:
                    small[stage]()
                else:
                    big[stage](k)
        for cp in sends:
            cp.wait_send()
        def finish(q, _):
            cp_x(q).wait_send()
            cp_p(q).wait_send()
            cp_f(q).wait_send()
            return 0
        lax.fori_loop(0, NQ, finish, 0)

    V = pltpu.VMEM
    D = pltpu.SemaphoreType.DMA
    W2 = 2 * CQ
    scratch = [V((1024, 1024), bf16), V((1, 1024), f32), V((100, 1024), bf16), V((100, 1024), f32), V((1, 1024), f32), V((1, 100), f32), V((1024, W2), bf16),
               V((NQ, 1024, W2), bf16), V((128, 1024), bf16), V((1024, 128), bf16),
               V((1024, 128), f32), V((128, 128), f32), V((104, 1024), f32),
               V((NQ, 1024, W2), bf16), V((NQ, 1024, W2), f32),
               V((NQ, 104, W2), f32), V((NQ, 104, W2), f32), V((NQ, 104, W2), f32), V((NQ, 104, W2), f32),
               V((NQ, 128, W2), bf16), V((1024, 128), f32), V((1024, 1024), f32), V((128, 1024), f32)]
    scratch += [V((NC, half, 1024), f32), V((128, 512), f32), V((128, 512), f32),
                V((NC, 2, 3, 4 * pr, 512), f32), V((NC, 2, 4 * pr, 512), f32), V((NC, 2, 3, pr, 512), f32),
                V((NC, pr, 1024), f32), V((NC, 7, pr, 128), f32),
                V((7, 16, 512), f32), V((16, 512), f32), V((3, 16, 128), f32), V((4, 16, 128), f32)]
    scratch += [D((NQ, 2)), D((6,))] + [D((NQ,))] * 6
    for shp in ((n,), (n, 2, 3), (n, 2, 3), (n, 7), (n, 7), (n, 2, 3), (n, 2, 3), (n,), (7,), (3,), (3,), (3,), (7,)):
        scratch += [D(shp), D(shp)]
    vm = pl.BlockSpec(memory_space=pltpu.VMEM)
    hbm = pl.BlockSpec(memory_space=pl.ANY)
    return pl.pallas_call(kern,
        out_shape=(jax.ShapeDtypeStruct((2, 1024, 1024), bf16), jax.ShapeDtypeStruct((1024, 1024), f32), jax.ShapeDtypeStruct((128, 1024), f32)),
        in_specs=[pl.BlockSpec(memory_space=pltpu.HBM)] * 7, out_specs=[vm, vm, vm],
        scratch_shapes=scratch, name="fused",
        compiler_params=pltpu.CompilerParams(collective_id=3, has_side_effects=True, vmem_limit_bytes=44 * 2**20))


def place(ghs, ow, os):
    def kern(ghs, ow, os, gh, gw, go, gb, out, sem):
        out[...] = os[:100, :]
        cps = [pltpu.make_async_copy(ow, gw, sem.at[0]), pltpu.make_async_copy(out, go, sem.at[1]), pltpu.make_async_copy(ghs, gh, sem.at[2])]
        for cp in cps:
            cp.start()
        gb[...] = os[104:105, :]
        for cp in cps:
            cp.wait()
    vm = pl.BlockSpec(memory_space=pltpu.VMEM)
    hbm = pl.BlockSpec(memory_space=pl.ANY)
    return pl.pallas_call(kern, out_shape=(jax.ShapeDtypeStruct((2, 1024, 1024), bf16), jax.ShapeDtypeStruct((1024, 1024), f32),
                                           jax.ShapeDtypeStruct((100, 1024), f32), jax.ShapeDtypeStruct((1, 1024), f32)),
        in_specs=[vm, vm, vm], out_specs=[hbm, hbm, hbm, vm], scratch_shapes=[pltpu.VMEM((100, 1024), f32), pltpu.SemaphoreType.DMA((3,))], name="place",
        compiler_params=pltpu.CompilerParams(has_side_effects=True, vmem_limit_bytes=2**20))(ghs, ow, os)


def per_device(hidden, w_first, b_first, w_out, target, area, var_weight):
    members = hidden.shape[0] * lax.axis_size("mem")
    total = members * hidden.shape[2] * lax.axis_size("pts")
    scale = 1.0 / math.sqrt(total)
    eps_fair = 0.05 / members
    pair_coef = (1.0 - eps_fair) / (members * (members - 1))
    args = [pltpu.with_memory_space_constraint(a, pltpu.HBM) for a in (hidden, w_first, b_first[None], w_out, target, area[None], var_weight[None])]
    ghs, ow, os = make_kernel(members, pair_coef, scale)(*args)
    grad_hidden, grad_first, grad_out, grad_bias = place(ghs, ow, os)
    return (grad_hidden, grad_first, grad_out, grad_bias[0])


def solution(mesh):
    return jax.shard_map(
        per_device,
        mesh=mesh,
        in_specs=(P("mem", None, "pts"), P(), P(), P(), P(None, "pts"), P("pts"), P()),
        out_specs=(P("mem", None, "pts"), P(), P(), P()),
        check_vma=False,
    )
```
